32 devices in a mesh: grp: 2 (over x), ep: 16 (over z, y, core).
Axes of the slice: x: 2, y: 2, z: 4, core: 2. Of those that a mesh axis runs over, the one named last changes fastest.
Arguments:
- resid: bfloat16 [2048, 2048], P('ep', 'grp'), may hold values from -6 to 6
- query: bfloat16 [2048, 2048], P('ep', 'grp'), may hold values from -6 to 6
- key_new: bfloat16 [2048, 2048], P('ep', 'grp'), may hold values from -6 to 6
- value_new: bfloat16 [2048, 2048], P('ep', 'grp'), may hold values from -6 to 6
- cache_kv: bfloat16 [2, 16384, 2048], P(None, 'ep', 'grp'), may hold values from -6 to 6
- cache_len: int32 [16], replicated, may hold values from 1 to 1024, 4096 in all
- w_out: bfloat16 [2048, 2048], P('grp'), may hold values from -0.125 to 0.125
- norm_gain: bfloat16 [2048], replicated, may hold values from 0.099609375 to 1.8984375
- w_router: bfloat16 [2048, 16], replicated, may hold values from -7 to 7
- routes: int32 [2048, 4], P('ep'), may hold values from 0 to 15, all different within a row; in each aligned block of 128 rows (0 to 127, 128 to 255, ...) at most 64 rows name the same one
- w_gate_up: bfloat16 [16, 2, 2048, 1408], P('ep', None, None, 'grp'), may hold values from -0.125 to 0.125
- w_down: bfloat16 [16, 1408, 2048], P('ep', 'grp'), may hold values from -0.15625 to 0.15625
Outputs:
- after_attention: bfloat16 [2048, 2048], P('ep', 'grp')
- expert_mix: bfloat16 [2048, 2048], P('ep', 'grp')
The draws below stay inside these ranges and needn't reach their ends.
Inputs may be any that keep to these rules, and one draw needn't show every extreme that they name: `routes`: in each aligned block of 128 rows (one request's tokens), no expert is named by more than 64 of the pairs, and in every draw some expert is named by exactly 64. Request r's cache fills the first cache_len[r] rows of its slab, rows r * 1024 onward of cache_kv; the rest of the slab is unused; the lengths sum to 4096 and the longest is exactly 1024.
All inputs are finite; a program needn't handle non-finite values.
Results may differ from the reference program's by a relative error of at most 0.013.
Values may be sent and summed in bfloat16 or wider, within the bound.
A program may use at most 64 MiB of HBM per device.

```python
import math
import jax
import jax.numpy as jnp
import numpy as np
from jax import lax

D = 2048
HEADS = 16
HD = 128
FFE = 1408
TOP = 4
TOK_DEV = 128
CACHE_DEV = 1024
REQUESTS = 16
EXPERTS = 16
TOKENS = 2048
CACHE = 16384
CACHED = 4096
CAP = 64
SLICE = 704
N_GRP = 2
N_EP = 16


ROUTER_SPREAD = 0.5


def drawn_normal(key, salt, shape):
    return jnp.clip(jax.random.normal(jax.random.fold_in(key, salt), shape, jnp.float32), -6.0, 6.0)


def draw_query(key, part):
    values_drawn = drawn_normal(key, 1, (TOKENS, HEADS * HD))
    return values_drawn.astype(jnp.bfloat16)


def draw_key_new(key, part):
    values_drawn = drawn_normal(key, 2, (TOKENS, HEADS * HD))
    return values_drawn.astype(jnp.bfloat16)


def draw_resid(key, part):
    values_drawn = drawn_normal(key, 3, (TOKENS, D))
    return values_drawn.astype(jnp.bfloat16)


def draw_w_router(key, part):
    values_drawn = drawn_normal(key, 4, (D, EXPERTS)) * (ROUTER_SPREAD * float(D) ** (-0.5))
    return values_drawn.astype(jnp.bfloat16)


def shard_levels(rng, extent, cuts, low, top_value):
    loudness, own = 1.0, jax.random.fold_in(rng, 6)
    for axis_at, shards_of in cuts:
        heights = jnp.exp(jax.random.uniform(jax.random.fold_in(own, axis_at), (shards_of,), jnp.float32, low / len(cuts), top_value / len(cuts)))
        loudness = loudness * jnp.repeat(heights, extent[axis_at] // shards_of).reshape([-1 if axis == axis_at else 1 for axis in range(len(extent))])
    return loudness


def length_profile(amount, total, most, lean):
    portions = [(1 << 20) // math.isqrt(grade ** lean) + 1 for grade in range(2, amount + 1)]
    surplus, counts = total - most - (amount - 1), [1] * (amount - 1)
    while surplus > 0:
        free = [i for i in range(amount - 1) if counts[i] < most]
        mass, left = sum([portions[i] for i in free]), surplus
        for i in free:
            extra = min(most - counts[i], max(1, left * portions[i] // mass), surplus)
            counts[i] = counts[i] + extra
            surplus = surplus - extra
    return np.array([most] + counts)


def ragged_sizes(own_key, number_of, total, bound, lean):
    if number_of == 2:
        one = jax.random.randint(own_key, (), max(1, total - bound), min(bound, total - 1) + 1)
        return jnp.stack([one, total - one])
    sizes = jnp.asarray(length_profile(number_of, total, bound, lean), jnp.int32)
    couples = (number_of - 1) // 2
    source_of, taker = sizes[1:1 + 2 * couples:2], sizes[2:2 + 2 * couples:2]
    margin = jnp.minimum(source_of - 1, bound - taker)
    shifted = jax.random.randint(jax.random.fold_in(own_key, 1), (couples,), 0, 1 << 20) % (margin + 1)
    sizes = sizes.at[1:1 + 2 * couples:2].set(source_of - shifted).at[2:2 + 2 * couples:2].set(taker + shifted)
    return sizes[jax.random.permutation(jax.random.fold_in(own_key, 2), number_of)]


def assign_block(key, own, number, rows, amount, top, bound, lean):
    ranking = jax.random.permutation(key, amount)
    crowded, ordinary = portions_of(amount, rows * top, bound, lean, True), portions_of(amount, rows * top, bound, lean, False)
    places = jnp.arange(amount)

    def named(sizes, turn):
        used = int((sizes > 0).sum())
        fixed = max(1, used // 4)
        passed = fixed + (places - fixed + turn * (used - fixed)) % max(1, amount - fixed)
        return jnp.zeros((amount,), jnp.int32).at[ranking[jnp.where(places < fixed, places, passed)]].set(jnp.asarray(sizes, jnp.int32))

    sizes = jnp.where(number % 4 == 0, named(crowded, number // 4), named(ordinary, number - number // 4 - 1))
    mixed = jax.random.permutation(jax.random.fold_in(own, 3), amount)
    giver, taker = mixed[0:amount // 2 * 2:2], mixed[1:amount // 2 * 2:2]
    margin = jnp.minimum(sizes[giver] - 1, bound - sizes[taker]) // 2
    margin = jnp.where((giver == ranking[0]) | (taker == ranking[0]) | (sizes[taker] == 0), 0, jnp.maximum(margin, 0))
    passed = jax.random.randint(jax.random.fold_in(own, 4), (amount // 2,), 0, 1 << 20) % (margin + 1)
    sizes = sizes.at[giver].add(-passed).at[taker].add(passed)
    members = jnp.searchsorted(jnp.cumsum(sizes), jnp.arange(rows * top), side="right").astype(jnp.int32)
    table = members.reshape(top, rows).T
    table = table[jax.random.permutation(jax.random.fold_in(own, 1), rows)]
    turn = jax.random.randint(jax.random.fold_in(own, 2), (rows, 1), 0, top)
    return jnp.take_along_axis(table, (jnp.arange(top)[None, :] + turn) % top, axis=1)


def portions_of(amount, total, most, lean, full):
    loads = [(1 << 20) // math.isqrt(rank ** lean) + 1 for rank in range(1, amount + 1)]
    largest = most if full else min(most, max(-(-total // amount), total * loads[0] // sum(loads)))
    least = 1 if total - largest >= amount - 1 else 0
    holding, spare = [largest] + [least] * (amount - 1), total - largest - least * (amount - 1)
    while spare > 0:
        free = [i for i in range(1, amount) if holding[i] < largest] or [i for i in range(1, amount) if holding[i] < most]
        pool, left = sum([loads[i] for i in free]), spare
        for i in free:
            addition = min(most - holding[i], max(1, left * loads[i] // pool), spare)
            holding[i] = holding[i] + addition
            spare = spare - addition
    return np.array(holding)


def gaussian(stream_key, shape, spread, bound, cuts=(), kind=jnp.bfloat16):
    drawn = jax.random.normal(stream_key, shape, jnp.float32) * spread
    if len(cuts) > 0:
        drawn = shard_levels(stream_key, shape, cuts, -0.22, 0.18) * drawn
    return jnp.clip(drawn, min=-bound, max=bound).astype(kind)


def setup_inputs(seed: int = 0) -> dict:
    splits = jax.random.split(jax.random.key(seed), 13)
    resid = draw_resid(jax.random.fold_in(splits[12], 71), 0)
    query = draw_query(jax.random.fold_in(splits[12], 71), 0)
    key_new = draw_key_new(jax.random.fold_in(splits[12], 71), 0)
    value_new = gaussian(splits[3], (TOKENS, HEADS * HD), 1.0, 6.0, ((0, 16), (1, 2)))
    cache_kv = gaussian(splits[4], (2, CACHE, HEADS * HD), 1.0, 6.0, ((1, 16), (2, 2)))
    cache_len = ragged_sizes(splits[5], REQUESTS, CACHED, CACHE_DEV, 2).astype(jnp.int32)
    w_out = gaussian(splits[6], (HEADS * HD, D), (HEADS * HD) ** -0.5, 0.125, ((0, 2),))
    norm_gain = jnp.clip(1.0 + 0.18 * jax.random.normal(splits[7], (D,), jnp.float32), 0.099609375, 1.8984375).astype(jnp.bfloat16)
    w_router = draw_w_router(jax.random.fold_in(splits[12], 71), 0)
    routes_keys = jax.random.split(jax.random.fold_in(splits[9], 1), TOKENS // TOK_DEV)
    routes_turns = jax.random.permutation(jax.random.fold_in(splits[9], 3), TOKENS // TOK_DEV)
    routes = jax.vmap(lambda own, number: assign_block(jax.random.fold_in(splits[9], 2), own, number, TOK_DEV, EXPERTS, TOP, CAP, 2))(routes_keys, routes_turns).reshape((TOKENS, TOP))
    w_gate_up = gaussian(splits[10], (EXPERTS, 2, D, FFE), D ** -0.5, 0.125, ((0, 16), (3, 2)))
    w_down = gaussian(splits[11], (EXPERTS, FFE, D), FFE ** -0.5, 0.15625, ((0, 16), (1, 2)))
    return {"resid": resid, "query": query, "key_new": key_new, "value_new": value_new, "cache_kv": cache_kv, "cache_len": cache_len, "w_out": w_out, "norm_gain": norm_gain, "w_router": w_router, "routes": routes, "w_gate_up": w_gate_up, "w_down": w_down}


EPS = 1e-06
MASKED = -1e+30

def attend(queries, new_keys, new_values, cache_keys, cache_values, length):
    score_scale = float(HD) ** (-0.5)
    queries = queries.astype(jnp.float32)
    new_keys = new_keys.astype(jnp.float32)
    new_values = new_values.astype(jnp.float32)
    cache_keys = cache_keys.astype(jnp.float32)
    cache_values = cache_values.astype(jnp.float32)
    position = jnp.arange(TOK_DEV, dtype=jnp.int32)
    new_scores = jnp.einsum('qhd,khd->qhk', queries, new_keys) * score_scale
    causal = (position[:, None] >= position[None, :])[:, None, :]
    new_scores = jnp.where(causal, new_scores, MASKED)
    cache_position = jnp.arange(CACHE_DEV, dtype=jnp.int32)
    live_rows = cache_position < length
    old_scores = jnp.einsum('qhd,khd->qhk', queries, cache_keys) * score_scale
    old_scores = jnp.where(live_rows[None, None, :], old_scores, MASKED)
    row_max = jnp.maximum(lax.optimization_barrier(jnp.max(new_scores, axis=-1)), lax.optimization_barrier(jnp.max(old_scores, axis=-1)))
    new_probs = jnp.exp(new_scores - row_max[..., None])
    old_probs = jnp.exp(old_scores - row_max[..., None])
    denominator = lax.optimization_barrier(jnp.sum(new_probs, axis=-1)) + lax.optimization_barrier(jnp.sum(old_probs, axis=-1))
    new_rounded = lax.optimization_barrier(new_probs.astype(jnp.bfloat16)).astype(jnp.float32)
    old_rounded = lax.optimization_barrier(old_probs.astype(jnp.bfloat16)).astype(jnp.float32)
    weighted = jnp.einsum('qhk,khd->qhd', new_rounded, new_values) + jnp.einsum('qhk,khd->qhd', old_rounded, cache_values)
    return (weighted / denominator[..., None]).astype(jnp.bfloat16)

def reference(resid, query, key_new, value_new, cache_kv, cache_len, w_out, norm_gain, w_router, routes, w_gate_up, w_down):
    shaped = (REQUESTS, TOK_DEV, HEADS, HD)
    queries = query.reshape(shaped)
    new_keys = key_new.reshape(shaped)
    new_values = value_new.reshape(shaped)
    slabs = cache_kv.reshape(2, REQUESTS, CACHE_DEV, HEADS, HD)
    lengths = cache_len.astype(jnp.int32)

    def one_request(inputs):
        request_q, request_k, request_v, slab_keys, slab_values, length = inputs
        return attend(request_q, request_k, request_v, slab_keys, slab_values, length)
    attended = lax.map(one_request, (queries, new_keys, new_values, slabs[0], slabs[1], lengths))
    attended = attended.reshape(TOKENS, HEADS * HD)
    projected = jnp.dot(attended, w_out, preferred_element_type=jnp.float32)
    after_attention = (resid.astype(jnp.float32) + projected).astype(jnp.bfloat16)
    after_wide = after_attention.astype(jnp.float32)
    inverse = lax.rsqrt(lax.optimization_barrier(jnp.mean(after_wide * after_wide, axis=1)) + EPS)
    normed = (after_wide * inverse[:, None] * norm_gain.astype(jnp.float32)[None, :]).astype(jnp.bfloat16)
    logits = jnp.dot(normed, w_router, preferred_element_type=jnp.float32)
    chosen = jnp.take_along_axis(logits, routes.astype(jnp.int32), axis=1)
    route_weight = jax.nn.softmax(chosen, axis=-1).astype(jnp.bfloat16)
    pairs = routes.astype(jnp.int32).reshape(N_EP, TOK_DEV * TOP)
    route_hits = (pairs[:, :, None] == jnp.arange(EXPERTS, dtype=jnp.int32)[None, None, :]).astype(jnp.int32)
    earlier = jnp.cumsum(route_hits, axis=1) - route_hits
    slot_index = lax.optimization_barrier(jnp.sum(earlier * route_hits, axis=2))
    block_index = jnp.arange(N_EP, dtype=jnp.int32)[:, None]
    row_id = (pairs * (N_EP * CAP) + block_index * CAP + slot_index).reshape(-1).astype(jnp.int32)
    sources = jnp.repeat(normed, TOP, axis=0)
    expert_input = jnp.zeros((EXPERTS * N_EP * CAP, D), jnp.bfloat16).at[row_id].set(sources)
    expert_input = expert_input.reshape(EXPERTS, N_EP * CAP, D)

    def one_expert(inputs):
        rows_in, gate_up, down_rows = inputs
        gate_value = jnp.dot(rows_in, gate_up[0], preferred_element_type=jnp.float32)
        up_value = jnp.dot(rows_in, gate_up[1], preferred_element_type=jnp.float32)
        hidden = (jax.nn.silu(gate_value) * up_value).astype(jnp.bfloat16)
        summed = jnp.zeros((rows_in.shape[0], D), jnp.float32)
        for group_number in range(N_GRP):
            partial_value = jnp.dot(hidden[:, group_number * SLICE:(group_number + 1) * SLICE], down_rows[group_number * SLICE:(group_number + 1) * SLICE], preferred_element_type=jnp.float32).astype(jnp.bfloat16)
            summed = summed + lax.optimization_barrier(partial_value).astype(jnp.float32)
        return summed
    expert_out = lax.map(one_expert, (expert_input, w_gate_up, w_down)).reshape(EXPERTS * N_EP * CAP, D)
    picked = expert_out[row_id].reshape(TOKENS, TOP, D)
    expert_mix = lax.optimization_barrier(jnp.sum(picked * route_weight.astype(jnp.float32)[:, :, None], axis=1))
    return (after_attention, expert_mix.astype(jnp.bfloat16))
```

```python
import jax
import jax.numpy as jnp
from jax import lax
from jax.experimental import pallas as pl
from jax.experimental.pallas import tpu as pltpu
from jax.sharding import PartitionSpec as P

D = 2048
HD = 128
TOP = 4


EPS = 1e-06
MASKED = -1e30


def expert_rows(arrived, w_gate_up, w_down):
    features = arrived.shape[-1]
    flat_rows = arrived.reshape(-1, features)
    gate_value = jnp.dot(flat_rows, w_gate_up[0, 0], preferred_element_type=jnp.float32)
    up_value = jnp.dot(flat_rows, w_gate_up[0, 1], preferred_element_type=jnp.float32)
    hidden = (jax.nn.silu(gate_value) * up_value).astype(jnp.bfloat16)
    partial_value = jnp.dot(hidden, w_down[0], preferred_element_type=jnp.float32).astype(
        jnp.bfloat16
    )
    return partial_value.reshape(arrived.shape)


def send_back(answered):
    return lax.all_to_all(answered, "ep", split_axis=0, concat_axis=0, tiled=True)


def wide_body(
    resid,
    query,
    key_new,
    value_new,
    cache_kv,
    cache_len,
    w_out,
    norm_gain,
    w_router,
    routes,
    w_gate_up,
    w_down,
):
    tokens_here = query.shape[0]
    heads_here = query.shape[1] // HD
    experts_all = w_router.shape[1]
    column_width = resid.shape[1]
    group_index = lax.axis_index("grp")
    request = lax.axis_index("ep")
    capacity = max(2, 8 * tokens_here // lax.axis_size("ep"))
    score_scale = float(HD) ** (-0.5)
    column_start = group_index * column_width
    queries = query.reshape(tokens_here, heads_here, HD)
    new_keys = key_new.reshape(tokens_here, heads_here, HD)
    new_values = value_new.reshape(tokens_here, heads_here, HD)
    cache_rows = cache_kv.shape[1]
    cache_keys = cache_kv[0].reshape(cache_rows, heads_here, HD)
    cache_values = cache_kv[1].reshape(cache_rows, heads_here, HD)
    own_length = lax.dynamic_index_in_dim(cache_len, request, 0, keepdims=False)
    position = jnp.arange(tokens_here, dtype=jnp.int32)
    causal = (position[:, None] >= position[None, :])[:, None, :]
    new_scores = (
        jnp.einsum("qhd,khd->qhk", queries, new_keys, preferred_element_type=jnp.float32)
        * score_scale
    )
    new_scores = jnp.where(causal, new_scores, MASKED)
    live_rows = (jnp.arange(cache_rows, dtype=jnp.int32) < own_length)[None, None, :]
    old_scores = (
        jnp.einsum("qhd,khd->qhk", queries, cache_keys, preferred_element_type=jnp.float32)
        * score_scale
    )
    old_scores = jnp.where(live_rows, old_scores, MASKED)
    row_max = jnp.maximum(jnp.max(new_scores, axis=-1), jnp.max(old_scores, axis=-1))
    new_probs = jnp.exp(new_scores - row_max[..., None])
    old_probs = jnp.exp(old_scores - row_max[..., None])
    denominator = jnp.sum(new_probs, axis=-1) + jnp.sum(old_probs, axis=-1)
    weighted = jnp.einsum(
        "qhk,khd->qhd",
        new_probs.astype(jnp.bfloat16),
        new_values,
        preferred_element_type=jnp.float32,
    )
    weighted = weighted + jnp.einsum(
        "qhk,khd->qhd",
        old_probs.astype(jnp.bfloat16),
        cache_values,
        preferred_element_type=jnp.float32,
    )
    attended = (
        (weighted / denominator[..., None])
        .astype(jnp.bfloat16)
        .reshape(tokens_here, heads_here * HD)
    )
    projected = jnp.dot(attended, w_out, preferred_element_type=jnp.float32)
    attn_share = lax.psum_scatter(projected, "grp", scatter_dimension=1, tiled=True)
    after_cols = (resid.astype(jnp.float32) + attn_share).astype(jnp.bfloat16)
    after_wide = after_cols.astype(jnp.float32)
    squares = lax.psum(jnp.sum(after_wide * after_wide, axis=1), "grp")
    inverse = lax.rsqrt(squares / D + EPS)
    gain_cols = lax.dynamic_slice_in_dim(norm_gain, column_start, column_width, 0)
    normed_cols = (after_wide * inverse[:, None] * gain_cols.astype(jnp.float32)[None, :]).astype(
        jnp.bfloat16
    )
    router_cols = lax.dynamic_slice_in_dim(w_router, column_start, column_width, 0)
    logits = lax.psum(jnp.dot(normed_cols, router_cols, preferred_element_type=jnp.float32), "grp")
    normed_full = lax.all_gather(normed_cols, "grp", axis=1, tiled=True)
    route_hits = routes[:, :, None] == jnp.arange(experts_all, dtype=jnp.int32)[None, None, :]
    chosen = jnp.sum(jnp.where(route_hits, logits[:, None, :], 0.0), axis=-1)
    route_weight = jax.nn.softmax(chosen, axis=-1).astype(jnp.bfloat16)
    flat_hits = route_hits.reshape(tokens_here * TOP, experts_all).astype(jnp.int32)
    earlier = jnp.cumsum(flat_hits, axis=0) - flat_hits
    slot_index = jnp.sum(earlier * flat_hits, axis=1)
    slot_row = (routes.reshape(-1) * capacity + slot_index).reshape(tokens_here, TOP)
    slot_ids = jnp.arange(experts_all * capacity, dtype=jnp.int32)
    matches = slot_row[:, :, None] == slot_ids[None, None, :]
    selection = jnp.any(matches, axis=1).astype(jnp.bfloat16)
    combine = jnp.sum(
        jnp.where(matches, route_weight[:, :, None], jnp.zeros((), jnp.bfloat16)), axis=1
    )
    outgoing = jnp.einsum(
        "tj,td->jd", selection, normed_full, preferred_element_type=jnp.float32
    ).astype(jnp.bfloat16)
    outgoing = outgoing.reshape(experts_all, capacity, D)
    returned = send_back(
        expert_rows(
            lax.all_to_all(outgoing, "ep", split_axis=0, concat_axis=0, tiled=True),
            w_gate_up,
            w_down,
        )
    )
    mixed_part = jnp.dot(
        combine, returned.reshape(experts_all * capacity, D), preferred_element_type=jnp.float32
    )
    mixed_cols = lax.psum_scatter(mixed_part, "grp", scatter_dimension=1, tiled=True)
    return (after_cols, mixed_cols.astype(jnp.bfloat16))


FIRST = 80
BATCH = 4


def exchange_kernel(
    normed_ref,
    slots_ref,
    router_ref,
    gate_up_hbm,
    down_hbm,
    out_ref,
    tokens,
    partial,
    from_core,
    from_x,
    from_x_last,
    from_y,
    from_y_last,
    from_z,
    from_z_last,
    gate_up,
    down,
    rows_in,
    hidden,
    combine,
    weight_sem,
    send_sem,
    recv_sem,
):
    count = normed_ref.shape[0]
    width = normed_ref.shape[1]
    capacity = combine.shape[1]
    experts = router_ref.shape[0]
    here = lax.axis_index("grp")
    there = 1 - here
    place = lax.axis_index("ep")
    core = lax.rem(place, 2)
    y_at = lax.rem(lax.div(place, 2), 2)
    z_low = lax.rem(lax.div(place, 4), 2)
    z_high = lax.div(place, 8)

    def moved(dz, dy, dc):
        high = 1 - z_high if dz // 2 else z_high
        low = 1 - z_low if dz % 2 else z_low
        along_y = 1 - y_at if dy else y_at
        on_core = 1 - core if dc else core
        return ((high * 2 + low) * 2 + along_y) * 2 + on_core

    by_x = (there, place)
    by_y = (here, moved(0, 1, 0))
    by_core = (here, moved(0, 0, 1))
    by_z = [None] + [(here, moved(dz, 0, 0)) for dz in (1, 2, 3)]

    weights = [
        pltpu.make_async_copy(gate_up_hbm.at[0], gate_up, weight_sem.at[0]),
        pltpu.make_async_copy(down_hbm.at[0], down, weight_sem.at[1]),
    ]
    for one in weights:
        one.start()

    barrier = pltpu.get_barrier_semaphore()
    peers = [by_x, by_y, by_core] + by_z[1:]
    for peer in peers:
        pl.semaphore_signal(barrier, inc=1, device_id=peer, device_id_type=pl.DeviceIdType.MESH)

    tokens[0, here] = normed_ref[...]
    pl.semaphore_wait(barrier, len(peers))

    first = pl.ds(0, FIRST)
    last = pl.ds(FIRST, count - FIRST)
    started = []

    def send(source, target, peer):
        index = len(started)
        copy = pltpu.make_async_remote_copy(
            src_ref=source,
            dst_ref=target,
            send_sem=send_sem.at[index],
            recv_sem=recv_sem.at[index],
            device_id=peer,
            device_id_type=pl.DeviceIdType.MESH,
        )
        copy.start()
        started.append(copy)
        return copy

    def gather_x(slot):
        piece = tokens.at[slot, here, first]
        return send(piece, piece, by_x)

    def gather_y(dz):
        return send(tokens.at[dz, here, first], tokens.at[4 + dz, here, first], by_y)

    def gather_y_last(dz):
        return send(tokens.at[dz, :, last], tokens.at[4 + dz, :, last], by_y)

    def gather_core(slot):
        return send(tokens.at[slot], tokens.at[8 + slot], by_core)

    x_last = send(tokens.at[0, here, last], tokens.at[0, here, last], by_x)
    z_first = [None] + [
        send(tokens.at[0, here, first], tokens.at[dz, here, first], by_z[dz]) for dz in (1, 2, 3)
    ]
    y_first = [gather_y(0)]
    x_first = [gather_x(0)]
    x_last.wait_recv()
    z_last = [None] + [
        send(tokens.at[0, :, last], tokens.at[dz, :, last], by_z[dz]) for dz in (1, 2, 3)
    ]
    y_last = [gather_y_last(0)]
    for dz in (1, 2, 3):
        z_first[dz].wait_recv()
        y_first.append(gather_y(dz))
        x_first.append(gather_x(dz))
    x_first[0].wait_recv()
    to_core = [gather_core(0)]
    for dz in (1, 2, 3):
        z_last[dz].wait_recv()
        y_last.append(gather_y_last(dz))
    for dz in range(4):
        y_first[dz].wait_recv()
        x_first.append(gather_x(4 + dz))
    for dz in (1, 2, 3):
        x_first[dz].wait_recv()
        to_core.append(gather_core(dz))

    expert_row = lax.broadcasted_iota(jnp.int32, (experts, count), 0) == place
    slot_row = lax.broadcasted_iota(jnp.int32, (capacity, count), 0)

    def experts_on(base):
        for step in range(BATCH):
            slot = base + step
            request = moved(slot % 4, (slot // 4) % 2, slot // 8)
            slots = slots_ref[request]
            halves = [tokens[slot, 0], tokens[slot, 1]]
            logits = sum(
                lax.dot_general(
                    router_ref[:, half * width : (half + 1) * width],
                    halves[half],
                    (((1,), (1,)), ((), ())),
                    preferred_element_type=jnp.float32,
                )
                for half in (0, 1)
            )
            logits = jnp.where(slots >= 0.0, logits, MASKED)
            raised = jnp.exp(logits - jnp.max(logits, axis=0, keepdims=True))
            share = raised / jnp.sum(raised, axis=0, keepdims=True)
            weight = jnp.sum(jnp.where(expert_row, share, 0.0), axis=0, keepdims=True)
            mine = jnp.sum(jnp.where(expert_row, slots, 0.0), axis=0, keepdims=True)
            chosen = slot_row == mine.astype(jnp.int32)
            combine[step] = jnp.where(chosen, weight, 0.0).astype(jnp.bfloat16)
            select = jnp.where(chosen, 1.0, 0.0).astype(jnp.bfloat16)
            for half in (0, 1):
                rows_in[step * capacity : (step + 1) * capacity, half * width : (half + 1) * width] = (
                    jnp.dot(select, halves[half], preferred_element_type=jnp.float32).astype(
                        jnp.bfloat16
                    )
                )
        units = hidden.shape[1]
        for start in range(0, units, 256):
            stop = min(start + 256, units)
            gate_value = jnp.dot(
                rows_in[...], gate_up[0, :, start:stop], preferred_element_type=jnp.float32
            )
            up_value = jnp.dot(
                rows_in[...], gate_up[1, :, start:stop], preferred_element_type=jnp.float32
            )
            hidden[:, start:stop] = (gate_value / (1.0 + jnp.exp(-gate_value)) * up_value).astype(
                jnp.bfloat16
            )
        for half in (0, 1):
            for start in range(0, width, 512):
                stop = min(start + 512, width)
                answered = jnp.dot(
                    hidden[...],
                    down[:, half * width + start : half * width + stop],
                    preferred_element_type=jnp.float32,
                ).astype(jnp.bfloat16)
                for step in range(BATCH):
                    partial[base + step, half, :, start:stop] = lax.dot_general(
                        combine[step],
                        answered[step * capacity : (step + 1) * capacity],
                        (((0,), (0,)), ((), ())),
                        preferred_element_type=jnp.float32,
                    ).astype(jnp.bfloat16)

    def added(one, other):
        return (one.astype(jnp.float32) + other.astype(jnp.float32)).astype(jnp.bfloat16)

    def return_core(slot):
        return send(partial.at[8 + slot], from_core.at[slot], by_core)

    def return_x(slot):
        return send(partial.at[slot, there, first], from_x.at[slot], by_x)

    for one in weights:
        one.wait()
    experts_on(0)
    for dz in range(4):
        to_core[dz].wait_recv()
    experts_on(8)
    back_core = [return_core(dz) for dz in range(4)]
    for dz in range(4):
        x_first[4 + dz].wait_recv()
        y_last[dz].wait_recv()
        to_core.append(gather_core(4 + dz))
    back_x = []
    for dz in range(4):
        back_core[dz].wait_recv()
        partial[dz] = added(partial[dz], from_core[dz])
        back_x.append(return_x(dz))
    for dz in range(4):
        to_core[4 + dz].wait_recv()
    experts_on(12)
    back_core += [return_core(4 + dz) for dz in range(4)]
    experts_on(4)
    back_y_last = []
    for dz in range(4):
        back_core[4 + dz].wait_recv()
        partial[4 + dz] = added(partial[4 + dz], from_core[4 + dz])
        back_y_last.append(send(partial.at[4 + dz, :, last], from_y_last.at[dz], by_y))
        back_x.append(return_x(4 + dz))
    back_y = []
    for dz in range(4):
        back_x[4 + dz].wait_recv()
        partial[4 + dz, here, :FIRST] = added(partial[4 + dz, here, :FIRST], from_x[4 + dz])
        back_y.append(send(partial.at[4 + dz, here, first], from_y.at[dz], by_y))
    back_z_last = [None]
    for dz in (1, 2, 3):
        back_y_last[dz].wait_recv()
        partial[dz, :, FIRST:] = added(partial[dz, :, FIRST:], from_y_last[dz])
        back_z_last.append(send(partial.at[dz, :, last], from_z_last.at[dz - 1], by_z[dz]))
    back_z = [None]
    for dz in (1, 2, 3):
        back_x[dz].wait_recv()
        back_y[dz].wait_recv()
        partial[dz, here, :FIRST] = (
            partial[dz, here, :FIRST].astype(jnp.float32)
            + from_x[dz].astype(jnp.float32)
            + from_y[dz].astype(jnp.float32)
        ).astype(jnp.bfloat16)
        back_z.append(send(partial.at[dz, here, first], from_z.at[dz - 1], by_z[dz]))
    back_y_last[0].wait_recv()
    for dz in (1, 2, 3):
        back_z_last[dz].wait_recv()

    def last_sum(half):
        total = partial[0, half, FIRST:].astype(jnp.float32) + from_y_last[0, half].astype(
            jnp.float32
        )
        for dz in (1, 2, 3):
            total = total + from_z_last[dz - 1, half].astype(jnp.float32)
        return total

    partial[0, there, FIRST:] = last_sum(there).astype(jnp.bfloat16)
    back_x_last = send(partial.at[0, there, last], from_x_last, by_x)
    back_x[0].wait_recv()
    back_y[0].wait_recv()
    for dz in (1, 2, 3):
        back_z[dz].wait_recv()
    total = (
        partial[0, here, :FIRST].astype(jnp.float32)
        + from_x[0].astype(jnp.float32)
        + from_y[0].astype(jnp.float32)
    )
    for dz in (1, 2, 3):
        total = total + from_z[dz - 1].astype(jnp.float32)
    out_ref[:FIRST] = total.astype(jnp.bfloat16)
    total = last_sum(here)
    back_x_last.wait_recv()
    out_ref[FIRST:] = (total + from_x_last[...].astype(jnp.float32)).astype(jnp.bfloat16)
    for copy in started:
        copy.wait_send()


def exchange(normed_cols, slots, router_rows, w_gate_up, w_down, capacity):
    count, width = normed_cols.shape
    units = w_gate_up.shape[-1]
    rest = count - FIRST
    low = jnp.bfloat16
    vmem = pl.BlockSpec(memory_space=pltpu.VMEM)
    hbm = pl.BlockSpec(memory_space=pl.ANY)
    return pl.pallas_call(
        exchange_kernel,
        out_shape=jax.ShapeDtypeStruct((count, width), low),
        in_specs=[vmem, vmem, vmem, hbm, hbm],
        out_specs=vmem,
        scratch_shapes=[
            pltpu.VMEM((16, 2, count, width), low),
            pltpu.VMEM((16, 2, count, width), low),
            pltpu.VMEM((8, 2, count, width), low),
            pltpu.VMEM((8, FIRST, width), low),
            pltpu.VMEM((rest, width), low),
            pltpu.VMEM((4, FIRST, width), low),
            pltpu.VMEM((4, 2, rest, width), low),
            pltpu.VMEM((3, FIRST, width), low),
            pltpu.VMEM((3, 2, rest, width), low),
            pltpu.VMEM((2, 2 * width, units), low),
            pltpu.VMEM((units, 2 * width), low),
            pltpu.VMEM((BATCH * capacity, 2 * width), low),
            pltpu.VMEM((BATCH * capacity, units), low),
            pltpu.VMEM((BATCH, capacity, count), low),
            pltpu.SemaphoreType.DMA((2,)),
            pltpu.SemaphoreType.DMA((62,)),
            pltpu.SemaphoreType.DMA((62,)),
        ],
        compiler_params=pltpu.CompilerParams(
            collective_id=0, has_side_effects=True, vmem_limit_bytes=56 * 1024 * 1024
        ),
        cost_estimate=pl.CostEstimate(
            flops=10_000_000_000, bytes_accessed=10_000_000, transcendentals=1_000_000
        ),
    )(normed_cols, slots, router_rows, w_gate_up, w_down)


def slot_table(routes, experts_all):
    tokens_here = routes.shape[0]
    hits = jnp.any(
        routes[None, :, :] == jnp.arange(experts_all, dtype=jnp.int32)[:, None, None], axis=2
    )
    position = jnp.arange(tokens_here, dtype=jnp.int32)
    earlier = (position[:, None] < position[None, :]).astype(jnp.bfloat16)
    slots = jnp.dot(hits.astype(jnp.bfloat16), earlier, preferred_element_type=jnp.float32)
    return jnp.where(hits, slots, -1.0)


def routed_body(
    resid,
    query,
    key_new,
    value_new,
    cache_kv,
    cache_len,
    w_out,
    norm_gain,
    w_router,
    routes,
    w_gate_up,
    w_down,
):
    tokens_here = query.shape[0]
    heads_here = query.shape[1] // HD
    experts_all = w_router.shape[1]
    column_width = resid.shape[1]
    table = lax.all_gather(slot_table(routes, experts_all), "ep", axis=0, tiled=False)
    group_index = lax.axis_index("grp")
    request = lax.axis_index("ep")
    capacity = max(2, 8 * tokens_here // lax.axis_size("ep"))
    score_scale = float(HD) ** (-0.5)
    column_start = group_index * column_width
    queries = query.reshape(tokens_here, heads_here, HD)
    new_keys = key_new.reshape(tokens_here, heads_here, HD)
    new_values = value_new.reshape(tokens_here, heads_here, HD)
    cache_rows = cache_kv.shape[1]
    cache_keys = cache_kv[0].reshape(cache_rows, heads_here, HD)
    cache_values = cache_kv[1].reshape(cache_rows, heads_here, HD)
    own_length = lax.dynamic_index_in_dim(cache_len, request, 0, keepdims=False)
    position = jnp.arange(tokens_here, dtype=jnp.int32)
    causal = (position[:, None] >= position[None, :])[:, None, :]
    new_scores = (
        jnp.einsum("qhd,khd->qhk", queries, new_keys, preferred_element_type=jnp.float32)
        * score_scale
    )
    new_scores = jnp.where(causal, new_scores, MASKED)
    live_rows = (jnp.arange(cache_rows, dtype=jnp.int32) < own_length)[None, None, :]
    old_scores = (
        jnp.einsum("qhd,khd->qhk", queries, cache_keys, preferred_element_type=jnp.float32)
        * score_scale
    )
    old_scores = jnp.where(live_rows, old_scores, MASKED)
    row_max = jnp.maximum(jnp.max(new_scores, axis=-1), jnp.max(old_scores, axis=-1))
    new_probs = jnp.exp(new_scores - row_max[..., None])
    old_probs = jnp.exp(old_scores - row_max[..., None])
    denominator = jnp.sum(new_probs, axis=-1) + jnp.sum(old_probs, axis=-1)
    weighted = jnp.einsum(
        "qhk,khd->qhd",
        new_probs.astype(jnp.bfloat16),
        new_values,
        preferred_element_type=jnp.float32,
    )
    weighted = weighted + jnp.einsum(
        "qhk,khd->qhd",
        old_probs.astype(jnp.bfloat16),
        cache_values,
        preferred_element_type=jnp.float32,
    )
    attended = (
        (weighted / denominator[..., None])
        .astype(jnp.bfloat16)
        .reshape(tokens_here, heads_here * HD)
    )
    projected = jnp.dot(attended, w_out, preferred_element_type=jnp.float32)
    attn_share = lax.psum_scatter(projected, "grp", scatter_dimension=1, tiled=True)
    after_cols = (resid.astype(jnp.float32) + attn_share).astype(jnp.bfloat16)
    after_wide = after_cols.astype(jnp.float32)
    squares = lax.psum(jnp.sum(after_wide * after_wide, axis=1), "grp")
    inverse = lax.rsqrt(squares / D + EPS)
    gain_cols = lax.dynamic_slice_in_dim(norm_gain, column_start, column_width, 0)
    normed_cols = (after_wide * inverse[:, None] * gain_cols.astype(jnp.float32)[None, :]).astype(
        jnp.bfloat16
    )
    mixed_cols = exchange(normed_cols, table, w_router.T, w_gate_up, w_down, capacity)
    return (after_cols, mixed_cols)


def solution(mesh):
    fits = mesh.shape["ep"] == 16 and mesh.shape["grp"] == 2
    return jax.shard_map(
        routed_body if fits else wide_body,
        mesh=mesh,
        in_specs=(
            P("ep", "grp"),
            P("ep", "grp"),
            P("ep", "grp"),
            P("ep", "grp"),
            P(None, "ep", "grp"),
            P(),
            P("grp", None),
            P(),
            P(),
            P("ep", None),
            P("ep", None, None, "grp"),
            P("ep", "grp", None),
        ),
        out_specs=(P("ep", "grp"), P("ep", "grp")),
        check_vma=False,
    )
```

```python
import jax
import jax.numpy as jnp
from jax import lax
from jax.experimental import pallas as pl
from jax.experimental.pallas import tpu as pltpu
from jax.sharding import PartitionSpec as P

D = 2048
HD = 128
TOP = 4


EPS = 1e-06
MASKED = -1e30


def expert_rows(arrived, w_gate_up, w_down):
    features = arrived.shape[-1]
    flat_rows = arrived.reshape(-1, features)
    gate_value = jnp.dot(flat_rows, w_gate_up[0, 0], preferred_element_type=jnp.float32)
    up_value = jnp.dot(flat_rows, w_gate_up[0, 1], preferred_element_type=jnp.float32)
    hidden = (jax.nn.silu(gate_value) * up_value).astype(jnp.bfloat16)
    partial_value = jnp.dot(hidden, w_down[0], preferred_element_type=jnp.float32).astype(
        jnp.bfloat16
    )
    return partial_value.reshape(arrived.shape)


def send_back(answered):
    return lax.all_to_all(answered, "ep", split_axis=0, concat_axis=0, tiled=True)


def wide_body(
    resid,
    query,
    key_new,
    value_new,
    cache_kv,
    cache_len,
    w_out,
    norm_gain,
    w_router,
    routes,
    w_gate_up,
    w_down,
):
    tokens_here = query.shape[0]
    heads_here = query.shape[1] // HD
    experts_all = w_router.shape[1]
    column_width = resid.shape[1]
    group_index = lax.axis_index("grp")
    request = lax.axis_index("ep")
    capacity = max(2, 8 * tokens_here // lax.axis_size("ep"))
    score_scale = float(HD) ** (-0.5)
    column_start = group_index * column_width
    queries = query.reshape(tokens_here, heads_here, HD)
    new_keys = key_new.reshape(tokens_here, heads_here, HD)
    new_values = value_new.reshape(tokens_here, heads_here, HD)
    cache_rows = cache_kv.shape[1]
    cache_keys = cache_kv[0].reshape(cache_rows, heads_here, HD)
    cache_values = cache_kv[1].reshape(cache_rows, heads_here, HD)
    own_length = lax.dynamic_index_in_dim(cache_len, request, 0, keepdims=False)
    position = jnp.arange(tokens_here, dtype=jnp.int32)
    causal = (position[:, None] >= position[None, :])[:, None, :]
    new_scores = (
        jnp.einsum("qhd,khd->qhk", queries, new_keys, preferred_element_type=jnp.float32)
        * score_scale
    )
    new_scores = jnp.where(causal, new_scores, MASKED)
    live_rows = (jnp.arange(cache_rows, dtype=jnp.int32) < own_length)[None, None, :]
    old_scores = (
        jnp.einsum("qhd,khd->qhk", queries, cache_keys, preferred_element_type=jnp.float32)
        * score_scale
    )
    old_scores = jnp.where(live_rows, old_scores, MASKED)
    row_max = jnp.maximum(jnp.max(new_scores, axis=-1), jnp.max(old_scores, axis=-1))
    new_probs = jnp.exp(new_scores - row_max[..., None])
    old_probs = jnp.exp(old_scores - row_max[..., None])
    denominator = jnp.sum(new_probs, axis=-1) + jnp.sum(old_probs, axis=-1)
    weighted = jnp.einsum(
        "qhk,khd->qhd",
        new_probs.astype(jnp.bfloat16),
        new_values,
        preferred_element_type=jnp.float32,
    )
    weighted = weighted + jnp.einsum(
        "qhk,khd->qhd",
        old_probs.astype(jnp.bfloat16),
        cache_values,
        preferred_element_type=jnp.float32,
    )
    attended = (
        (weighted / denominator[..., None])
        .astype(jnp.bfloat16)
        .reshape(tokens_here, heads_here * HD)
    )
    projected = jnp.dot(attended, w_out, preferred_element_type=jnp.float32)
    attn_share = lax.psum_scatter(projected, "grp", scatter_dimension=1, tiled=True)
    after_cols = (resid.astype(jnp.float32) + attn_share).astype(jnp.bfloat16)
    after_wide = after_cols.astype(jnp.float32)
    squares = lax.psum(jnp.sum(after_wide * after_wide, axis=1), "grp")
    inverse = lax.rsqrt(squares / D + EPS)
    gain_cols = lax.dynamic_slice_in_dim(norm_gain, column_start, column_width, 0)
    normed_cols = (after_wide * inverse[:, None] * gain_cols.astype(jnp.float32)[None, :]).astype(
        jnp.bfloat16
    )
    router_cols = lax.dynamic_slice_in_dim(w_router, column_start, column_width, 0)
    logits = lax.psum(jnp.dot(normed_cols, router_cols, preferred_element_type=jnp.float32), "grp")
    normed_full = lax.all_gather(normed_cols, "grp", axis=1, tiled=True)
    route_hits = routes[:, :, None] == jnp.arange(experts_all, dtype=jnp.int32)[None, None, :]
    chosen = jnp.sum(jnp.where(route_hits, logits[:, None, :], 0.0), axis=-1)
    route_weight = jax.nn.softmax(chosen, axis=-1).astype(jnp.bfloat16)
    flat_hits = route_hits.reshape(tokens_here * TOP, experts_all).astype(jnp.int32)
    earlier = jnp.cumsum(flat_hits, axis=0) - flat_hits
    slot_index = jnp.sum(earlier * flat_hits, axis=1)
    slot_row = (routes.reshape(-1) * capacity + slot_index).reshape(tokens_here, TOP)
    slot_ids = jnp.arange(experts_all * capacity, dtype=jnp.int32)
    matches = slot_row[:, :, None] == slot_ids[None, None, :]
    selection = jnp.any(matches, axis=1).astype(jnp.bfloat16)
    combine = jnp.sum(
        jnp.where(matches, route_weight[:, :, None], jnp.zeros((), jnp.bfloat16)), axis=1
    )
    outgoing = jnp.einsum(
        "tj,td->jd", selection, normed_full, preferred_element_type=jnp.float32
    ).astype(jnp.bfloat16)
    outgoing = outgoing.reshape(experts_all, capacity, D)
    returned = send_back(
        expert_rows(
            lax.all_to_all(outgoing, "ep", split_axis=0, concat_axis=0, tiled=True),
            w_gate_up,
            w_down,
        )
    )
    mixed_part = jnp.dot(
        combine, returned.reshape(experts_all * capacity, D), preferred_element_type=jnp.float32
    )
    mixed_cols = lax.psum_scatter(mixed_part, "grp", scatter_dimension=1, tiled=True)
    return (after_cols, mixed_cols.astype(jnp.bfloat16))


FIRST = 80
BATCH = 4


def layer_kernel(
    length_ref,
    resid_ref,
    query_ref,
    key_ref,
    value_ref,
    gain_ref,
    slots_ref,
    router_ref,
    cache_hbm,
    project_hbm,
    gate_up_hbm,
    down_hbm,
    after_ref,
    out_ref,
    cache,
    project,
    attended,
    share_out,
    share_in,
    squares_out,
    squares_in,
    slots_all,
    tokens,
    partial,
    from_core,
    from_x,
    from_x_last,
    from_y,
    from_y_last,
    from_z,
    from_z_last,
    gate_up,
    down,
    rows_in,
    hidden,
    combine,
    weight_sem,
    send_sem,
    recv_sem,
):
    count, width = resid_ref.shape
    capacity = combine.shape[1]
    experts = router_ref.shape[0]
    here = lax.axis_index("grp")
    there = 1 - here
    place = lax.axis_index("ep")
    core = lax.rem(place, 2)
    y_at = lax.rem(lax.div(place, 2), 2)
    z_low = lax.rem(lax.div(place, 4), 2)
    z_high = lax.div(place, 8)

    def moved(dz, dy, dc):
        high = 1 - z_high if dz // 2 else z_high
        low = 1 - z_low if dz % 2 else z_low
        along_y = 1 - y_at if dy else y_at
        on_core = 1 - core if dc else core
        return ((high * 2 + low) * 2 + along_y) * 2 + on_core

    by_x = (there, place)
    by_y = (here, moved(0, 1, 0))
    by_core = (here, moved(0, 0, 1))
    by_z = [None] + [(here, moved(dz, 0, 0)) for dz in (1, 2, 3)]

    keys = pltpu.make_async_copy(cache_hbm.at[0], cache.at[0], weight_sem.at[0])
    values = pltpu.make_async_copy(cache_hbm.at[1], cache.at[1], weight_sem.at[1])
    projection = [
        pltpu.make_async_copy(
            project_hbm.at[:, half * width : (half + 1) * width],
            project.at[half],
            weight_sem.at[2 + half],
        )
        for half in (0, 1)
    ]
    weights = [
        pltpu.make_async_copy(gate_up_hbm.at[0], gate_up, weight_sem.at[4]),
        pltpu.make_async_copy(down_hbm.at[0], down, weight_sem.at[5]),
    ]
    for one in [keys, values] + projection + weights:
        one.start()

    barrier = pltpu.get_barrier_semaphore()
    peers = [by_x, by_y, by_core] + by_z[1:]
    for peer in peers:
        pl.semaphore_signal(barrier, inc=1, device_id=peer, device_id_type=pl.DeviceIdType.MESH)

    slots_all[0] = slots_ref[...]
    pl.semaphore_wait(barrier, len(peers))

    first = pl.ds(0, FIRST)
    last = pl.ds(FIRST, count - FIRST)
    started = []

    def send(source, target, peer):
        index = len(started)
        copy = pltpu.make_async_remote_copy(
            src_ref=source,
            dst_ref=target,
            send_sem=send_sem.at[index],
            recv_sem=recv_sem.at[index],
            device_id=peer,
            device_id_type=pl.DeviceIdType.MESH,
        )
        copy.start()
        started.append(copy)
        return copy

    def gather_x(slot):
        piece = tokens.at[slot, here, first]
        return send(piece, piece, by_x)

    def gather_y(dz):
        return send(tokens.at[dz, here, first], tokens.at[4 + dz, here, first], by_y)

    def gather_y_last(dz):
        return send(tokens.at[dz, :, last], tokens.at[4 + dz, :, last], by_y)

    def gather_core(slot):
        return send(tokens.at[slot], tokens.at[8 + slot], by_core)

    slots_z = [
        send(slots_all.at[0], slots_all.at[dz], by_z[dz]) for dz in (1, 2, 3)
    ]
    slots_y = [send(slots_all.at[0], slots_all.at[4], by_y)]

    score_scale = float(HD) ** (-0.5)
    live_rows = (
        lax.broadcasted_iota(jnp.int32, (count, cache.shape[1]), 1) < length_ref[place]
    )
    causal = lax.broadcasted_iota(jnp.int32, (count, count), 0) >= lax.broadcasted_iota(
        jnp.int32, (count, count), 1
    )
    along_last = (((1,), (1,)), ((), ()))
    keys.wait()
    values.wait()
    for start in range(0, width, HD):
        columns = slice(start, start + HD)
        asked = query_ref[:, columns]
        new_scores = score_scale * lax.dot_general(
            asked, key_ref[:, columns], along_last, preferred_element_type=jnp.float32
        )
        old_scores = score_scale * lax.dot_general(
            asked, cache[0, :, columns], along_last, preferred_element_type=jnp.float32
        )
        new_scores = jnp.where(causal, new_scores, MASKED)
        old_scores = jnp.where(live_rows, old_scores, MASKED)
        row_max = jnp.maximum(
            jnp.max(new_scores, axis=1, keepdims=True), jnp.max(old_scores, axis=1, keepdims=True)
        )
        new_probs = jnp.exp(new_scores - row_max)
        old_probs = jnp.exp(old_scores - row_max)
        denominator = jnp.sum(new_probs, axis=1, keepdims=True) + jnp.sum(
            old_probs, axis=1, keepdims=True
        )
        weighted = jnp.dot(
            new_probs.astype(jnp.bfloat16),
            value_ref[:, columns],
            preferred_element_type=jnp.float32,
        ) + jnp.dot(
            old_probs.astype(jnp.bfloat16),
            cache[1, :, columns],
            preferred_element_type=jnp.float32,
        )
        attended[:, columns] = (weighted / denominator).astype(jnp.bfloat16)

    for one in projection:
        one.wait()
    share_out[...] = jnp.dot(
        attended[...], project[there], preferred_element_type=jnp.float32
    ).astype(jnp.bfloat16)
    share = send(share_out, share_in, by_x)
    for dz in (1, 2, 3):
        slots_z[dz - 1].wait_recv()
        slots_y.append(send(slots_all.at[dz], slots_all.at[4 + dz], by_y))
    own_share = jnp.dot(attended[...], project[here], preferred_element_type=jnp.float32)
    slots_core = [send(slots_all.at[dz], slots_all.at[8 + dz], by_core) for dz in range(4)]
    for dz in range(4):
        slots_y[dz].wait_recv()
        slots_core.append(send(slots_all.at[4 + dz], slots_all.at[12 + dz], by_core))
    share.wait_recv()
    after = (
        resid_ref[...].astype(jnp.float32) + (own_share + share_in[...].astype(jnp.float32))
    ).astype(jnp.bfloat16)
    after_ref[...] = after
    after = after.astype(jnp.float32)
    squares = jnp.sum(after * after, axis=1, keepdims=True)
    squares_out[...] = jnp.transpose(jnp.broadcast_to(squares, (count, 128)))[:8]
    squares_sent = send(squares_out, squares_in, by_x)
    squares_sent.wait_recv()
    squares = squares + jnp.transpose(jnp.broadcast_to(squares_in[:1], (128, count)))[:, :1]
    inverse = lax.rsqrt(squares / (2 * width) + EPS)
    tokens[0, here] = (after * inverse * gain_ref[here].astype(jnp.float32)).astype(jnp.bfloat16)

    x_last = send(tokens.at[0, here, last], tokens.at[0, here, last], by_x)
    y_first = [gather_y(0)]
    x_first = {0: gather_x(0)}
    z_first = [None]
    z_last = [None]
    y_last = []
    to_core = {}
    z_first.append(send(tokens.at[0, here, first], tokens.at[1, here, first], by_z[1]))
    x_last.wait_recv()
    for dz in (1, 2, 3):
        if dz > 1:
            z_first.append(send(tokens.at[0, here, first], tokens.at[dz, here, first], by_z[dz]))
        z_last.append(send(tokens.at[0, :, last], tokens.at[dz, :, last], by_z[dz]))
    y_last.append(gather_y_last(0))

    def arrive_z(dz):
        z_first[dz].wait_recv()
        y_first.append(gather_y(dz))
        x_first[dz] = gather_x(dz)
        z_last[dz].wait_recv()
        y_last.append(gather_y_last(dz))

    def arrive_y(dz):
        y_first[dz].wait_recv()
        x_first[4 + dz] = gather_x(4 + dz)
        x_first[dz].wait_recv()
        to_core[dz] = gather_core(dz)

    def arrive_x(dz):
        x_first[4 + dz].wait_recv()
        y_last[dz].wait_recv()
        to_core[4 + dz] = gather_core(4 + dz)

    expert_row = lax.broadcasted_iota(jnp.int32, (experts, count), 0) == place
    slot_row = lax.broadcasted_iota(jnp.int32, (capacity, count), 0)

    def experts_on(dz):
        for step in range(BATCH):
            slot = dz + 4 * step
            slots = slots_all[slot]
            halves = [tokens[slot, 0], tokens[slot, 1]]
            logits = sum(
                lax.dot_general(
                    router_ref[:, half * width : (half + 1) * width],
                    halves[half],
                    along_last,
                    preferred_element_type=jnp.float32,
                )
                for half in (0, 1)
            )
            logits = jnp.where(slots >= 0.0, logits, MASKED)
            raised = jnp.exp(logits - jnp.max(logits, axis=0, keepdims=True))
            share = raised / jnp.sum(raised, axis=0, keepdims=True)
            weight = jnp.sum(jnp.where(expert_row, share, 0.0), axis=0, keepdims=True)
            mine = jnp.sum(jnp.where(expert_row, slots, 0.0), axis=0, keepdims=True)
            chosen = slot_row == mine.astype(jnp.int32)
            combine[step] = jnp.where(chosen, weight, 0.0).astype(jnp.bfloat16)
            select = jnp.where(chosen, 1.0, 0.0).astype(jnp.bfloat16)
            for half in (0, 1):
                rows_in[step * capacity : (step + 1) * capacity, half * width : (half + 1) * width] = (
                    jnp.dot(select, halves[half], preferred_element_type=jnp.float32).astype(
                        jnp.bfloat16
                    )
                )
        units = hidden.shape[1]
        for start in range(0, units, 256):
            stop = min(start + 256, units)
            gate_value = lax.dot_general(
                rows_in[...],
                gate_up[0, start:stop],
                along_last,
                preferred_element_type=jnp.float32,
            )
            up_value = lax.dot_general(
                rows_in[...],
                gate_up[1, start:stop],
                along_last,
                preferred_element_type=jnp.float32,
            )
            hidden[:, start:stop] = (gate_value / (1.0 + jnp.exp(-gate_value)) * up_value).astype(
                jnp.bfloat16
            )
        for half in (0, 1):
            for start in range(0, width, 512):
                stop = min(start + 512, width)
                answered = jnp.dot(
                    hidden[...],
                    down[:, half * width + start : half * width + stop],
                    preferred_element_type=jnp.float32,
                ).astype(jnp.bfloat16)
                for step in range(BATCH):
                    partial[dz + 4 * step, half, :, start:stop] = lax.dot_general(
                        combine[step],
                        answered[step * capacity : (step + 1) * capacity],
                        (((0,), (0,)), ((), ())),
                        preferred_element_type=jnp.float32,
                    ).astype(jnp.bfloat16)

    def added(one, other):
        return (one.astype(jnp.float32) + other.astype(jnp.float32)).astype(jnp.bfloat16)

    def return_core(slot):
        return send(partial.at[8 + slot], from_core.at[slot], by_core)

    def return_x(slot):
        return send(partial.at[slot, there, first], from_x.at[slot], by_x)

    back_core = {}
    back_x = {}
    back_y = {}
    back_y_last = {}
    back_z = {}
    back_z_last = {}

    def answer(dz):
        to_core[dz].wait_recv()
        to_core[4 + dz].wait_recv()
        experts_on(dz)
        for slot in (4 + dz, dz):
            back_core[slot] = return_core(slot)

    def core_sum(dz):
        for slot in (4 + dz, dz):
            back_core[slot].wait_recv()
            partial[slot] = added(partial[slot], from_core[slot])
            back_x[slot] = return_x(slot)
            if slot >= 4:
                back_y_last[dz] = send(partial.at[slot, :, last], from_y_last.at[dz], by_y)

    def x_sum(dz):
        back_x[4 + dz].wait_recv()
        partial[4 + dz, here, :FIRST] = added(partial[4 + dz, here, :FIRST], from_x[4 + dz])
        back_y[dz] = send(partial.at[4 + dz, here, first], from_y.at[dz], by_y)

    def y_sum(dz):
        back_y_last[dz].wait_recv()
        partial[dz, :, FIRST:] = added(partial[dz, :, FIRST:], from_y_last[dz])
        back_z_last[dz] = send(partial.at[dz, :, last], from_z_last.at[dz - 1], by_z[dz])
        back_x[dz].wait_recv()
        back_y[dz].wait_recv()
        partial[dz, here, :FIRST] = (
            partial[dz, here, :FIRST].astype(jnp.float32)
            + from_x[dz].astype(jnp.float32)
            + from_y[dz].astype(jnp.float32)
        ).astype(jnp.bfloat16)
        back_z[dz] = send(partial.at[dz, here, first], from_z.at[dz - 1], by_z[dz])

    arrive_y(0)
    arrive_z(1)
    arrive_x(0)
    arrive_y(1)
    for one in slots_core:
        one.wait_recv()
    for one in weights:
        one.wait()
    answer(0)
    arrive_z(2)
    arrive_x(1)
    arrive_y(2)
    core_sum(0)
    answer(1)
    arrive_z(3)
    arrive_x(2)
    arrive_y(3)
    core_sum(1)
    x_sum(0)
    answer(2)
    arrive_x(3)
    x_sum(1)
    core_sum(2)
    y_sum(1)
    answer(3)
    x_sum(2)
    core_sum(3)
    y_sum(2)
    x_sum(3)
    y_sum(3)
    back_y_last[0].wait_recv()
    for dz in (1, 2, 3):
        back_z_last[dz].wait_recv()

    def last_sum(half):
        total = partial[0, half, FIRST:].astype(jnp.float32) + from_y_last[0, half].astype(
            jnp.float32
        )
        for dz in (1, 2, 3):
            total = total + from_z_last[dz - 1, half].astype(jnp.float32)
        return total

    partial[0, there, FIRST:] = last_sum(there).astype(jnp.bfloat16)
    back_x_last = send(partial.at[0, there, last], from_x_last, by_x)
    back_x[0].wait_recv()
    back_y[0].wait_recv()
    for dz in (1, 2, 3):
        back_z[dz].wait_recv()
    total = (
        partial[0, here, :FIRST].astype(jnp.float32)
        + from_x[0].astype(jnp.float32)
        + from_y[0].astype(jnp.float32)
    )
    for dz in (1, 2, 3):
        total = total + from_z[dz - 1].astype(jnp.float32)
    out_ref[:FIRST] = total.astype(jnp.bfloat16)
    total = last_sum(here)
    back_x_last.wait_recv()
    out_ref[FIRST:] = (total + from_x_last[...].astype(jnp.float32)).astype(jnp.bfloat16)
    for copy in started:
        copy.wait_send()


def layer(
    lengths,
    resid,
    query,
    key_new,
    value_new,
    gain,
    slots,
    router_rows,
    cache_kv,
    w_out,
    gate_up_rows,
    w_down,
    capacity,
):
    count, width = resid.shape
    units = w_down.shape[1]
    rest = count - FIRST
    low = jnp.bfloat16
    wide = jnp.float32
    vmem = pl.BlockSpec(memory_space=pltpu.VMEM)
    hbm = pl.BlockSpec(memory_space=pl.ANY)
    block = jax.ShapeDtypeStruct((count, width), low)
    return pl.pallas_call(
        layer_kernel,
        out_shape=(block, block),
        in_specs=[pl.BlockSpec(memory_space=pltpu.SMEM)] + [vmem] * 7 + [hbm] * 4,
        out_specs=(vmem, vmem),
        scratch_shapes=[
            pltpu.VMEM(cache_kv.shape, low),
            pltpu.VMEM((2, width, width), low),
            pltpu.VMEM((count, width), low),
            pltpu.VMEM((count, width), low),
            pltpu.VMEM((count, width), low),
            pltpu.VMEM((8, count), wide),
            pltpu.VMEM((8, count), wide),
            pltpu.VMEM((16,) + slots.shape, wide),
            pltpu.VMEM((16, 2, count, width), low),
            pltpu.VMEM((16, 2, count, width), low),
            pltpu.VMEM((8, 2, count, width), low),
            pltpu.VMEM((8, FIRST, width), low),
            pltpu.VMEM((rest, width), low),
            pltpu.VMEM((4, FIRST, width), low),
            pltpu.VMEM((4, 2, rest, width), low),
            pltpu.VMEM((3, FIRST, width), low),
            pltpu.VMEM((3, 2, rest, width), low),
            pltpu.VMEM((2, units, 2 * width), low),
            pltpu.VMEM((units, 2 * width), low),
            pltpu.VMEM((BATCH * capacity, 2 * width), low),
            pltpu.VMEM((BATCH * capacity, units), low),
            pltpu.VMEM((BATCH, capacity, count), low),
            pltpu.SemaphoreType.DMA((6,)),
            pltpu.SemaphoreType.DMA((79,)),
            pltpu.SemaphoreType.DMA((79,)),
        ],
        compiler_params=pltpu.CompilerParams(
            collective_id=0, has_side_effects=True, vmem_limit_bytes=60 * 1024 * 1024
        ),
        cost_estimate=pl.CostEstimate(
            flops=12_000_000_000, bytes_accessed=18_000_000, transcendentals=2_000_000
        ),
    )(
        lengths,
        resid,
        query,
        key_new,
        value_new,
        gain,
        slots,
        router_rows,
        cache_kv,
        w_out,
        gate_up_rows,
        w_down,
    )


def slot_table(routes, experts_all):
    tokens_here = routes.shape[0]
    hits = jnp.any(
        routes.T[None, :, :] == jnp.arange(experts_all, dtype=jnp.int32)[:, None, None], axis=1
    )
    position = jnp.arange(tokens_here, dtype=jnp.int32)
    earlier = (position[:, None] < position[None, :]).astype(jnp.bfloat16)
    slots = jnp.dot(hits.astype(jnp.bfloat16), earlier, preferred_element_type=jnp.float32)
    return jnp.where(hits, slots, -1.0)


def routed_body(
    resid,
    query,
    key_new,
    value_new,
    cache_kv,
    cache_len,
    w_out,
    norm_gain,
    w_router,
    routes,
    w_gate_up,
    w_down,
):
    experts_all = w_router.shape[1]
    width = resid.shape[1]
    capacity = max(2, 8 * resid.shape[0] // lax.axis_size("ep"))
    return layer(
        cache_len,
        resid,
        query,
        key_new,
        value_new,
        norm_gain.reshape(2, 1, width),
        slot_table(routes, experts_all),
        w_router.T,
        cache_kv,
        w_out,
        jnp.swapaxes(w_gate_up, 2, 3),
        w_down,
        capacity,
    )


def solution(mesh):
    fits = mesh.shape["ep"] == 16 and mesh.shape["grp"] == 2
    return jax.shard_map(
        routed_body if fits else wide_body,
        mesh=mesh,
        in_specs=(
            P("ep", "grp"),
            P("ep", "grp"),
            P("ep", "grp"),
            P("ep", "grp"),
            P(None, "ep", "grp"),
            P(),
            P("grp", None),
            P(),
            P(),
            P("ep", None),
            P("ep", None, None, "grp"),
            P("ep", "grp", None),
        ),
        out_specs=(P("ep", "grp"), P("ep", "grp")),
        check_vma=False,
    )
```

```python
import jax
import jax.numpy as jnp
from jax import lax
from jax.experimental import pallas as pl
from jax.experimental.pallas import tpu as pltpu
from jax.sharding import PartitionSpec as P

D = 2048
HD = 128
TOP = 4


EPS = 1e-06
MASKED = -1e30


def expert_rows(arrived, w_gate_up, w_down):
    features = arrived.shape[-1]
    flat_rows = arrived.reshape(-1, features)
    gate_value = jnp.dot(flat_rows, w_gate_up[0, 0], preferred_element_type=jnp.float32)
    up_value = jnp.dot(flat_rows, w_gate_up[0, 1], preferred_element_type=jnp.float32)
    hidden = (jax.nn.silu(gate_value) * up_value).astype(jnp.bfloat16)
    partial_value = jnp.dot(hidden, w_down[0], preferred_element_type=jnp.float32).astype(
        jnp.bfloat16
    )
    return partial_value.reshape(arrived.shape)


def send_back(answered):
    return lax.all_to_all(answered, "ep", split_axis=0, concat_axis=0, tiled=True)


def wide_body(
    resid,
    query,
    key_new,
    value_new,
    cache_kv,
    cache_len,
    w_out,
    norm_gain,
    w_router,
    routes,
    w_gate_up,
    w_down,
):
    tokens_here = query.shape[0]
    heads_here = query.shape[1] // HD
    experts_all = w_router.shape[1]
    column_width = resid.shape[1]
    group_index = lax.axis_index("grp")
    request = lax.axis_index("ep")
    capacity = max(2, 8 * tokens_here // lax.axis_size("ep"))
    score_scale = float(HD) ** (-0.5)
    column_start = group_index * column_width
    queries = query.reshape(tokens_here, heads_here, HD)
    new_keys = key_new.reshape(tokens_here, heads_here, HD)
    new_values = value_new.reshape(tokens_here, heads_here, HD)
    cache_rows = cache_kv.shape[1]
    cache_keys = cache_kv[0].reshape(cache_rows, heads_here, HD)
    cache_values = cache_kv[1].reshape(cache_rows, heads_here, HD)
    own_length = lax.dynamic_index_in_dim(cache_len, request, 0, keepdims=False)
    position = jnp.arange(tokens_here, dtype=jnp.int32)
    causal = (position[:, None] >= position[None, :])[:, None, :]
    new_scores = (
        jnp.einsum("qhd,khd->qhk", queries, new_keys, preferred_element_type=jnp.float32)
        * score_scale
    )
    new_scores = jnp.where(causal, new_scores, MASKED)
    live_rows = (jnp.arange(cache_rows, dtype=jnp.int32) < own_length)[None, None, :]
    old_scores = (
        jnp.einsum("qhd,khd->qhk", queries, cache_keys, preferred_element_type=jnp.float32)
        * score_scale
    )
    old_scores = jnp.where(live_rows, old_scores, MASKED)
    row_max = jnp.maximum(jnp.max(new_scores, axis=-1), jnp.max(old_scores, axis=-1))
    new_probs = jnp.exp(new_scores - row_max[..., None])
    old_probs = jnp.exp(old_scores - row_max[..., None])
    denominator = jnp.sum(new_probs, axis=-1) + jnp.sum(old_probs, axis=-1)
    weighted = jnp.einsum(
        "qhk,khd->qhd",
        new_probs.astype(jnp.bfloat16),
        new_values,
        preferred_element_type=jnp.float32,
    )
    weighted = weighted + jnp.einsum(
        "qhk,khd->qhd",
        old_probs.astype(jnp.bfloat16),
        cache_values,
        preferred_element_type=jnp.float32,
    )
    attended = (
        (weighted / denominator[..., None])
        .astype(jnp.bfloat16)
        .reshape(tokens_here, heads_here * HD)
    )
    projected = jnp.dot(attended, w_out, preferred_element_type=jnp.float32)
    attn_share = lax.psum_scatter(projected, "grp", scatter_dimension=1, tiled=True)
    after_cols = (resid.astype(jnp.float32) + attn_share).astype(jnp.bfloat16)
    after_wide = after_cols.astype(jnp.float32)
    squares = lax.psum(jnp.sum(after_wide * after_wide, axis=1), "grp")
    inverse = lax.rsqrt(squares / D + EPS)
    gain_cols = lax.dynamic_slice_in_dim(norm_gain, column_start, column_width, 0)
    normed_cols = (after_wide * inverse[:, None] * gain_cols.astype(jnp.float32)[None, :]).astype(
        jnp.bfloat16
    )
    router_cols = lax.dynamic_slice_in_dim(w_router, column_start, column_width, 0)
    logits = lax.psum(jnp.dot(normed_cols, router_cols, preferred_element_type=jnp.float32), "grp")
    normed_full = lax.all_gather(normed_cols, "grp", axis=1, tiled=True)
    route_hits = routes[:, :, None] == jnp.arange(experts_all, dtype=jnp.int32)[None, None, :]
    chosen = jnp.sum(jnp.where(route_hits, logits[:, None, :], 0.0), axis=-1)
    route_weight = jax.nn.softmax(chosen, axis=-1).astype(jnp.bfloat16)
    flat_hits = route_hits.reshape(tokens_here * TOP, experts_all).astype(jnp.int32)
    earlier = jnp.cumsum(flat_hits, axis=0) - flat_hits
    slot_index = jnp.sum(earlier * flat_hits, axis=1)
    slot_row = (routes.reshape(-1) * capacity + slot_index).reshape(tokens_here, TOP)
    slot_ids = jnp.arange(experts_all * capacity, dtype=jnp.int32)
    matches = slot_row[:, :, None] == slot_ids[None, None, :]
    selection = jnp.any(matches, axis=1).astype(jnp.bfloat16)
    combine = jnp.sum(
        jnp.where(matches, route_weight[:, :, None], jnp.zeros((), jnp.bfloat16)), axis=1
    )
    outgoing = jnp.einsum(
        "tj,td->jd", selection, normed_full, preferred_element_type=jnp.float32
    ).astype(jnp.bfloat16)
    outgoing = outgoing.reshape(experts_all, capacity, D)
    returned = send_back(
        expert_rows(
            lax.all_to_all(outgoing, "ep", split_axis=0, concat_axis=0, tiled=True),
            w_gate_up,
            w_down,
        )
    )
    mixed_part = jnp.dot(
        combine, returned.reshape(experts_all * capacity, D), preferred_element_type=jnp.float32
    )
    mixed_cols = lax.psum_scatter(mixed_part, "grp", scatter_dimension=1, tiled=True)
    return (after_cols, mixed_cols.astype(jnp.bfloat16))


FIRST = 80
BATCH = 4


def layer_kernel(
    length_ref,
    resid_ref,
    query_ref,
    key_ref,
    value_ref,
    gain_ref,
    slots_ref,
    router_ref,
    cache_hbm,
    project_hbm,
    gate_up_hbm,
    down_hbm,
    after_ref,
    out_ref,
    cache,
    project,
    attended,
    share_out,
    share_in,
    squares_out,
    squares_in,
    logits_out,
    logits_in,
    tables,
    tokens,
    partial,
    from_core,
    from_x,
    from_x_last,
    from_y,
    from_y_last,
    from_z,
    from_z_last,
    gate_up,
    down,
    rows_in,
    hidden,
    combine,
    weight_sem,
    send_sem,
    recv_sem,
):
    count, width = resid_ref.shape
    capacity = combine.shape[1]
    experts = router_ref.shape[0]
    here = lax.axis_index("grp")
    there = 1 - here
    place = lax.axis_index("ep")
    core = lax.rem(place, 2)
    y_at = lax.rem(lax.div(place, 2), 2)
    z_low = lax.rem(lax.div(place, 4), 2)
    z_high = lax.div(place, 8)

    def moved(dz, dy, dc):
        high = 1 - z_high if dz // 2 else z_high
        low = 1 - z_low if dz % 2 else z_low
        along_y = 1 - y_at if dy else y_at
        on_core = 1 - core if dc else core
        return ((high * 2 + low) * 2 + along_y) * 2 + on_core

    by_x = (there, place)
    by_y = (here, moved(0, 1, 0))
    by_core = (here, moved(0, 0, 1))
    by_z = [None] + [(here, moved(dz, 0, 0)) for dz in (1, 2, 3)]

    keys = pltpu.make_async_copy(cache_hbm.at[0], cache.at[0], weight_sem.at[0])
    values = pltpu.make_async_copy(cache_hbm.at[1], cache.at[1], weight_sem.at[1])
    projection = [
        pltpu.make_async_copy(
            project_hbm.at[:, half * width : (half + 1) * width],
            project.at[half],
            weight_sem.at[2 + half],
        )
        for half in (0, 1)
    ]
    weights = [
        pltpu.make_async_copy(gate_up_hbm.at[0], gate_up, weight_sem.at[4]),
        pltpu.make_async_copy(down_hbm.at[0], down, weight_sem.at[5]),
    ]
    for one in [keys, values] + projection + weights:
        one.start()

    barrier = pltpu.get_barrier_semaphore()
    peers = [by_x, by_y, by_core] + by_z[1:]
    for peer in peers:
        pl.semaphore_signal(barrier, inc=1, device_id=peer, device_id_type=pl.DeviceIdType.MESH)

    tables[0, 0] = slots_ref[...]
    pl.semaphore_wait(barrier, len(peers))

    first = pl.ds(0, FIRST)
    last = pl.ds(FIRST, count - FIRST)
    started = []

    def send(source, target, peer):
        index = len(started)
        copy = pltpu.make_async_remote_copy(
            src_ref=source,
            dst_ref=target,
            send_sem=send_sem.at[index],
            recv_sem=recv_sem.at[index],
            device_id=peer,
            device_id_type=pl.DeviceIdType.MESH,
        )
        copy.start()
        started.append(copy)
        return copy

    def gather_x(slot):
        piece = tokens.at[slot, here, first]
        return send(piece, piece, by_x)

    def gather_y(dz):
        return send(tokens.at[dz, here, first], tokens.at[4 + dz, here, first], by_y)

    def gather_y_last(dz):
        return send(tokens.at[dz, :, last], tokens.at[4 + dz, :, last], by_y)

    def gather_core(slot):
        return send(tokens.at[slot], tokens.at[8 + slot], by_core)

    score_scale = float(HD) ** (-0.5)
    live_rows = (
        lax.broadcasted_iota(jnp.int32, (count, cache.shape[1]), 1) < length_ref[place]
    )
    causal = lax.broadcasted_iota(jnp.int32, (count, count), 0) >= lax.broadcasted_iota(
        jnp.int32, (count, count), 1
    )
    along_last = (((1,), (1,)), ((), ()))
    keys.wait()
    values.wait()
    for start in range(0, width, HD):
        columns = slice(start, start + HD)
        asked = query_ref[:, columns]
        new_scores = score_scale * lax.dot_general(
            asked, key_ref[:, columns], along_last, preferred_element_type=jnp.float32
        )
        old_scores = score_scale * lax.dot_general(
            asked, cache[0, :, columns], along_last, preferred_element_type=jnp.float32
        )
        new_scores = jnp.where(causal, new_scores, MASKED)
        old_scores = jnp.where(live_rows, old_scores, MASKED)
        row_max = jnp.maximum(
            jnp.max(new_scores, axis=1, keepdims=True), jnp.max(old_scores, axis=1, keepdims=True)
        )
        new_probs = jnp.exp(new_scores - row_max)
        old_probs = jnp.exp(old_scores - row_max)
        denominator = jnp.sum(new_probs, axis=1, keepdims=True) + jnp.sum(
            old_probs, axis=1, keepdims=True
        )
        weighted = jnp.dot(
            new_probs.astype(jnp.bfloat16),
            value_ref[:, columns],
            preferred_element_type=jnp.float32,
        ) + jnp.dot(
            old_probs.astype(jnp.bfloat16),
            cache[1, :, columns],
            preferred_element_type=jnp.float32,
        )
        attended[:, columns] = (weighted / denominator).astype(jnp.bfloat16)

    for one in projection:
        one.wait()
    share_out[...] = jnp.dot(
        attended[...], project[there], preferred_element_type=jnp.float32
    ).astype(jnp.bfloat16)
    share = send(share_out, share_in, by_x)
    own_share = jnp.dot(attended[...], project[here], preferred_element_type=jnp.float32)
    share.wait_recv()
    after = (
        resid_ref[...].astype(jnp.float32) + (own_share + share_in[...].astype(jnp.float32))
    ).astype(jnp.bfloat16)
    after_ref[...] = after
    after = after.astype(jnp.float32)
    squares = jnp.sum(after * after, axis=1, keepdims=True)
    squares_out[...] = jnp.transpose(jnp.broadcast_to(squares, (count, 128)))[:8]
    squares_sent = send(squares_out, squares_in, by_x)
    squares_sent.wait_recv()
    squares = squares + jnp.transpose(jnp.broadcast_to(squares_in[:1], (128, count)))[:, :1]
    inverse = lax.rsqrt(squares / (2 * width) + EPS)
    half_here = pl.ds(pl.multiple_of(here * width, 128), width)
    normed = (after * inverse * gain_ref[:, half_here]).astype(jnp.bfloat16)
    tokens[0, here] = normed

    x_last = send(tokens.at[0, here, last], tokens.at[0, here, last], by_x)
    y_first = [gather_y(0)]
    x_first = {0: gather_x(0)}
    z_first = [None]
    z_last = [None]
    y_last = []
    to_core = {}
    z_first.append(send(tokens.at[0, here, first], tokens.at[1, here, first], by_z[1]))
    own_logits = lax.dot_general(
        router_ref[:, half_here], normed, along_last, preferred_element_type=jnp.float32
    )
    logits_out[...] = own_logits
    logits_sent = send(logits_out, logits_in, by_x)
    x_last.wait_recv()
    for dz in (1, 2, 3):
        if dz > 1:
            z_first.append(send(tokens.at[0, here, first], tokens.at[dz, here, first], by_z[dz]))
        z_last.append(send(tokens.at[0, :, last], tokens.at[dz, :, last], by_z[dz]))
    y_last.append(gather_y_last(0))
    logits_sent.wait_recv()
    logits = jnp.where(slots_ref[...] >= 0.0, own_logits + logits_in[...], MASKED)
    raised = jnp.exp(logits - jnp.max(logits, axis=0, keepdims=True))
    tables[0, 1] = raised / jnp.sum(raised, axis=0, keepdims=True)
    table_z = [None] + [send(tables.at[0], tables.at[dz], by_z[dz]) for dz in (1, 2, 3)]
    table_y = [send(tables.at[0], tables.at[4], by_y)]
    table_core = {0: send(tables.at[0], tables.at[8], by_core)}

    def arrive_z(dz):
        table_z[dz].wait_recv()
        table_y.append(send(tables.at[dz], tables.at[4 + dz], by_y))
        table_core[dz] = send(tables.at[dz], tables.at[8 + dz], by_core)
        z_first[dz].wait_recv()
        y_first.append(gather_y(dz))
        x_first[dz] = gather_x(dz)
        z_last[dz].wait_recv()
        y_last.append(gather_y_last(dz))

    def arrive_y(dz):
        table_y[dz].wait_recv()
        table_core[4 + dz] = send(tables.at[4 + dz], tables.at[12 + dz], by_core)
        y_first[dz].wait_recv()
        x_first[4 + dz] = gather_x(4 + dz)
        x_first[dz].wait_recv()
        to_core[dz] = gather_core(dz)

    def arrive_x(dz):
        x_first[4 + dz].wait_recv()
        y_last[dz].wait_recv()
        to_core[4 + dz] = gather_core(4 + dz)

    expert_row = lax.broadcasted_iota(jnp.int32, (experts, count), 0) == place
    slot_row = lax.broadcasted_iota(jnp.int32, (capacity, count), 0)
    units = hidden.shape[1]
    features = rows_in.shape[1]

    def rows_of(step):
        return slice(step * capacity, (step + 1) * capacity)

    def hidden_on(dz):
        for step in range(BATCH):
            slot = dz + 4 * step
            mine, weight = (
                jnp.sum(jnp.where(expert_row, tables[slot, part], 0.0), axis=0, keepdims=True)
                for part in (0, 1)
            )
            chosen = slot_row == mine.astype(jnp.int32)
            combine[step] = jnp.where(chosen, weight, 0.0).astype(jnp.bfloat16)
            select = jnp.where(chosen, 1.0, 0.0).astype(jnp.bfloat16)
            for half in (0, 1):
                rows_in[rows_of(step), half * width : (half + 1) * width] = jnp.dot(
                    select, tokens[slot, half], preferred_element_type=jnp.float32
                ).astype(jnp.bfloat16)
        for start in range(0, units, 256):
            stop = min(start + 256, units)
            gate_value, up_value = (
                lax.dot_general(
                    rows_in[...],
                    gate_up[part, start:stop],
                    along_last,
                    preferred_element_type=jnp.float32,
                )
                for part in (0, 1)
            )
            hidden[:, start:stop] = (gate_value / (1.0 + jnp.exp(-gate_value)) * up_value).astype(
                jnp.bfloat16
            )

    def answers_on(dz):
        for start in range(0, features, 512):
            stop = min(start + 512, features)
            rows_in[:, start:stop] = jnp.dot(
                hidden[...], down[:, start:stop], preferred_element_type=jnp.float32
            ).astype(jnp.bfloat16)
        for step in (3, 2, 1, 0):
            slot = dz + 4 * step
            for half in (0, 1):
                partial[slot, half] = lax.dot_general(
                    combine[step],
                    rows_in[rows_of(step), half * width : (half + 1) * width],
                    (((0,), (0,)), ((), ())),
                    preferred_element_type=jnp.float32,
                ).astype(jnp.bfloat16)
            if slot >= 8:
                back_core[slot - 8] = return_core(slot - 8)

    def added(one, other):
        return one + other

    def return_core(slot):
        return send(partial.at[8 + slot], from_core.at[slot], by_core)

    def return_x(slot):
        return send(partial.at[slot, there, first], from_x.at[slot], by_x)

    back_core = {}
    back_x = {}
    back_y = {}
    back_y_last = {}
    back_z = {}
    back_z_last = {}

    def answer_rows(dz):
        for slot in (dz, 4 + dz):
            table_core[slot].wait_recv()
            to_core[slot].wait_recv()
        hidden_on(dz)

    def core_sum(dz):
        for slot in (4 + dz, dz):
            back_core[slot].wait_recv()
            partial[slot] = added(partial[slot], from_core[slot])
            back_x[slot] = return_x(slot)
            if slot >= 4:
                back_y_last[dz] = send(partial.at[slot, :, last], from_y_last.at[dz], by_y)

    def x_sum(dz):
        back_x[4 + dz].wait_recv()
        partial[4 + dz, here, :FIRST] = added(partial[4 + dz, here, :FIRST], from_x[4 + dz])
        back_y[dz] = send(partial.at[4 + dz, here, first], from_y.at[dz], by_y)

    def y_sum(dz):
        back_y_last[dz].wait_recv()
        partial[dz, :, FIRST:] = added(partial[dz, :, FIRST:], from_y_last[dz])
        back_z_last[dz] = send(partial.at[dz, :, last], from_z_last.at[dz - 1], by_z[dz])
        back_x[dz].wait_recv()
        back_y[dz].wait_recv()
        partial[dz, here, :FIRST] = (
            partial[dz, here, :FIRST].astype(jnp.float32)
            + from_x[dz].astype(jnp.float32)
            + from_y[dz].astype(jnp.float32)
        ).astype(jnp.bfloat16)
        back_z[dz] = send(partial.at[dz, here, first], from_z.at[dz - 1], by_z[dz])

    arrive_y(0)
    arrive_z(1)
    arrive_x(0)
    arrive_y(1)
    for one in weights:
        one.wait()
    answer_rows(0)
    arrive_z(2)
    answers_on(0)
    arrive_x(1)
    arrive_y(2)
    answer_rows(1)
    arrive_z(3)
    answers_on(1)
    core_sum(0)
    arrive_x(2)
    arrive_y(3)
    answer_rows(2)
    core_sum(1)
    x_sum(0)
    answers_on(2)
    arrive_x(3)
    answer_rows(3)
    x_sum(1)
    core_sum(2)
    answers_on(3)
    y_sum(1)
    x_sum(2)
    core_sum(3)
    y_sum(2)
    x_sum(3)
    y_sum(3)
    back_y_last[0].wait_recv()
    for dz in (1, 2, 3):
        back_z_last[dz].wait_recv()

    def last_sum(half):
        total = partial[0, half, FIRST:].astype(jnp.float32) + from_y_last[0, half].astype(
            jnp.float32
        )
        for dz in (1, 2, 3):
            total = total + from_z_last[dz - 1, half].astype(jnp.float32)
        return total

    partial[0, there, FIRST:] = last_sum(there).astype(jnp.bfloat16)
    back_x_last = send(partial.at[0, there, last], from_x_last, by_x)
    back_x[0].wait_recv()
    back_y[0].wait_recv()
    for dz in (1, 2, 3):
        back_z[dz].wait_recv()
    total = (
        partial[0, here, :FIRST].astype(jnp.float32)
        + from_x[0].astype(jnp.float32)
        + from_y[0].astype(jnp.float32)
    )
    for dz in (1, 2, 3):
        total = total + from_z[dz - 1].astype(jnp.float32)
    out_ref[:FIRST] = total.astype(jnp.bfloat16)
    total = last_sum(here)
    back_x_last.wait_recv()
    out_ref[FIRST:] = (total + from_x_last[...].astype(jnp.float32)).astype(jnp.bfloat16)
    for copy in started:
        copy.wait_send()


def layer(
    lengths,
    resid,
    query,
    key_new,
    value_new,
    gain,
    slots,
    router_rows,
    cache_kv,
    w_out,
    gate_up_rows,
    w_down,
    capacity,
):
    count, width = resid.shape
    units = w_down.shape[1]
    rest = count - FIRST
    low = jnp.bfloat16
    wide = jnp.float32
    vmem = pl.BlockSpec(memory_space=pltpu.VMEM)
    hbm = pl.BlockSpec(memory_space=pl.ANY)
    block = jax.ShapeDtypeStruct((count, width), low)
    return pl.pallas_call(
        layer_kernel,
        out_shape=(block, block),
        in_specs=[pl.BlockSpec(memory_space=pltpu.SMEM)] + [vmem] * 7 + [hbm] * 4,
        out_specs=(vmem, vmem),
        scratch_shapes=[
            pltpu.VMEM(cache_kv.shape, low),
            pltpu.VMEM((2, width, width), low),
            pltpu.VMEM((count, width), low),
            pltpu.VMEM((count, width), low),
            pltpu.VMEM((count, width), low),
            pltpu.VMEM((8, count), wide),
            pltpu.VMEM((8, count), wide),
            pltpu.VMEM(slots.shape, wide),
            pltpu.VMEM(slots.shape, wide),
            pltpu.VMEM((16, 2) + slots.shape, wide),
            pltpu.VMEM((16, 2, count, width), low),
            pltpu.VMEM((16, 2, count, width), low),
            pltpu.VMEM((8, 2, count, width), low),
            pltpu.VMEM((8, FIRST, width), low),
            pltpu.VMEM((rest, width), low),
            pltpu.VMEM((4, FIRST, width), low),
            pltpu.VMEM((4, 2, rest, width), low),
            pltpu.VMEM((3, FIRST, width), low),
            pltpu.VMEM((3, 2, rest, width), low),
            pltpu.VMEM((2, units, 2 * width), low),
            pltpu.VMEM((units, 2 * width), low),
            pltpu.VMEM((BATCH * capacity, 2 * width), low),
            pltpu.VMEM((BATCH * capacity, units), low),
            pltpu.VMEM((BATCH, capacity, count), low),
            pltpu.SemaphoreType.DMA((6,)),
            pltpu.SemaphoreType.DMA((80,)),
            pltpu.SemaphoreType.DMA((80,)),
        ],
        compiler_params=pltpu.CompilerParams(
            collective_id=0, has_side_effects=True, vmem_limit_bytes=60 * 1024 * 1024
        ),
        cost_estimate=pl.CostEstimate(
            flops=12_000_000_000, bytes_accessed=18_000_000, transcendentals=2_000_000
        ),
    )(
        lengths,
        resid,
        query,
        key_new,
        value_new,
        gain,
        slots,
        router_rows,
        cache_kv,
        w_out,
        gate_up_rows,
        w_down,
    )


def slot_table(routes, experts_all):
    tokens_here = routes.shape[0]
    hits = jnp.any(
        routes.T[None, :, :] == jnp.arange(experts_all, dtype=jnp.int32)[:, None, None], axis=1
    )
    position = jnp.arange(tokens_here, dtype=jnp.int32)
    earlier = (position[:, None] < position[None, :]).astype(jnp.bfloat16)
    slots = jnp.dot(hits.astype(jnp.bfloat16), earlier, preferred_element_type=jnp.float32)
    return jnp.where(hits, slots, -1.0)


def routed_body(
    resid,
    query,
    key_new,
    value_new,
    cache_kv,
    cache_len,
    w_out,
    norm_gain,
    w_router,
    routes,
    w_gate_up,
    w_down,
):
    experts_all = w_router.shape[1]
    width = resid.shape[1]
    capacity = max(2, 8 * resid.shape[0] // lax.axis_size("ep"))
    return layer(
        cache_len,
        resid,
        query,
        key_new,
        value_new,
        norm_gain.astype(jnp.float32).reshape(1, 2 * width),
        slot_table(routes, experts_all),
        w_router.T,
        cache_kv,
        w_out,
        jnp.swapaxes(w_gate_up, 2, 3),
        w_down,
        capacity,
    )


def solution(mesh):
    fits = mesh.shape["ep"] == 16 and mesh.shape["grp"] == 2
    return jax.shard_map(
        routed_body if fits else wide_body,
        mesh=mesh,
        in_specs=(
            P("ep", "grp"),
            P("ep", "grp"),
            P("ep", "grp"),
            P("ep", "grp"),
            P(None, "ep", "grp"),
            P(),
            P("grp", None),
            P(),
            P(),
            P("ep", None),
            P("ep", None, None, "grp"),
            P("ep", "grp", None),
        ),
        out_specs=(P("ep", "grp"), P("ep", "grp")),
        check_vma=False,
    )
```

```python
import jax
import jax.numpy as jnp
from jax import lax
from jax.experimental import pallas as pl
from jax.experimental.pallas import tpu as pltpu
from jax.sharding import PartitionSpec as P

D = 2048
HD = 128
TOP = 4


EPS = 1e-06
MASKED = -1e30


def expert_rows(arrived, w_gate_up, w_down):
    features = arrived.shape[-1]
    flat_rows = arrived.reshape(-1, features)
    gate_value = jnp.dot(flat_rows, w_gate_up[0, 0], preferred_element_type=jnp.float32)
    up_value = jnp.dot(flat_rows, w_gate_up[0, 1], preferred_element_type=jnp.float32)
    hidden = (jax.nn.silu(gate_value) * up_value).astype(jnp.bfloat16)
    partial_value = jnp.dot(hidden, w_down[0], preferred_element_type=jnp.float32).astype(
        jnp.bfloat16
    )
    return partial_value.reshape(arrived.shape)


def send_back(answered):
    return lax.all_to_all(answered, "ep", split_axis=0, concat_axis=0, tiled=True)


def wide_body(
    resid,
    query,
    key_new,
    value_new,
    cache_kv,
    cache_len,
    w_out,
    norm_gain,
    w_router,
    routes,
    w_gate_up,
    w_down,
):
    tokens_here = query.shape[0]
    heads_here = query.shape[1] // HD
    experts_all = w_router.shape[1]
    column_width = resid.shape[1]
    group_index = lax.axis_index("grp")
    request = lax.axis_index("ep")
    capacity = max(2, 8 * tokens_here // lax.axis_size("ep"))
    score_scale = float(HD) ** (-0.5)
    column_start = group_index * column_width
    queries = query.reshape(tokens_here, heads_here, HD)
    new_keys = key_new.reshape(tokens_here, heads_here, HD)
    new_values = value_new.reshape(tokens_here, heads_here, HD)
    cache_rows = cache_kv.shape[1]
    cache_keys = cache_kv[0].reshape(cache_rows, heads_here, HD)
    cache_values = cache_kv[1].reshape(cache_rows, heads_here, HD)
    own_length = lax.dynamic_index_in_dim(cache_len, request, 0, keepdims=False)
    position = jnp.arange(tokens_here, dtype=jnp.int32)
    causal = (position[:, None] >= position[None, :])[:, None, :]
    new_scores = (
        jnp.einsum("qhd,khd->qhk", queries, new_keys, preferred_element_type=jnp.float32)
        * score_scale
    )
    new_scores = jnp.where(causal, new_scores, MASKED)
    live_rows = (jnp.arange(cache_rows, dtype=jnp.int32) < own_length)[None, None, :]
    old_scores = (
        jnp.einsum("qhd,khd->qhk", queries, cache_keys, preferred_element_type=jnp.float32)
        * score_scale
    )
    old_scores = jnp.where(live_rows, old_scores, MASKED)
    row_max = jnp.maximum(jnp.max(new_scores, axis=-1), jnp.max(old_scores, axis=-1))
    new_probs = jnp.exp(new_scores - row_max[..., None])
    old_probs = jnp.exp(old_scores - row_max[..., None])
    denominator = jnp.sum(new_probs, axis=-1) + jnp.sum(old_probs, axis=-1)
    weighted = jnp.einsum(
        "qhk,khd->qhd",
        new_probs.astype(jnp.bfloat16),
        new_values,
        preferred_element_type=jnp.float32,
    )
    weighted = weighted + jnp.einsum(
        "qhk,khd->qhd",
        old_probs.astype(jnp.bfloat16),
        cache_values,
        preferred_element_type=jnp.float32,
    )
    attended = (
        (weighted / denominator[..., None])
        .astype(jnp.bfloat16)
        .reshape(tokens_here, heads_here * HD)
    )
    projected = jnp.dot(attended, w_out, preferred_element_type=jnp.float32)
    attn_share = lax.psum_scatter(projected, "grp", scatter_dimension=1, tiled=True)
    after_cols = (resid.astype(jnp.float32) + attn_share).astype(jnp.bfloat16)
    after_wide = after_cols.astype(jnp.float32)
    squares = lax.psum(jnp.sum(after_wide * after_wide, axis=1), "grp")
    inverse = lax.rsqrt(squares / D + EPS)
    gain_cols = lax.dynamic_slice_in_dim(norm_gain, column_start, column_width, 0)
    normed_cols = (after_wide * inverse[:, None] * gain_cols.astype(jnp.float32)[None, :]).astype(
        jnp.bfloat16
    )
    router_cols = lax.dynamic_slice_in_dim(w_router, column_start, column_width, 0)
    logits = lax.psum(jnp.dot(normed_cols, router_cols, preferred_element_type=jnp.float32), "grp")
    normed_full = lax.all_gather(normed_cols, "grp", axis=1, tiled=True)
    route_hits = routes[:, :, None] == jnp.arange(experts_all, dtype=jnp.int32)[None, None, :]
    chosen = jnp.sum(jnp.where(route_hits, logits[:, None, :], 0.0), axis=-1)
    route_weight = jax.nn.softmax(chosen, axis=-1).astype(jnp.bfloat16)
    flat_hits = route_hits.reshape(tokens_here * TOP, experts_all).astype(jnp.int32)
    earlier = jnp.cumsum(flat_hits, axis=0) - flat_hits
    slot_index = jnp.sum(earlier * flat_hits, axis=1)
    slot_row = (routes.reshape(-1) * capacity + slot_index).reshape(tokens_here, TOP)
    slot_ids = jnp.arange(experts_all * capacity, dtype=jnp.int32)
    matches = slot_row[:, :, None] == slot_ids[None, None, :]
    selection = jnp.any(matches, axis=1).astype(jnp.bfloat16)
    combine = jnp.sum(
        jnp.where(matches, route_weight[:, :, None], jnp.zeros((), jnp.bfloat16)), axis=1
    )
    outgoing = jnp.einsum(
        "tj,td->jd", selection, normed_full, preferred_element_type=jnp.float32
    ).astype(jnp.bfloat16)
    outgoing = outgoing.reshape(experts_all, capacity, D)
    returned = send_back(
        expert_rows(
            lax.all_to_all(outgoing, "ep", split_axis=0, concat_axis=0, tiled=True),
            w_gate_up,
            w_down,
        )
    )
    mixed_part = jnp.dot(
        combine, returned.reshape(experts_all * capacity, D), preferred_element_type=jnp.float32
    )
    mixed_cols = lax.psum_scatter(mixed_part, "grp", scatter_dimension=1, tiled=True)
    return (after_cols, mixed_cols.astype(jnp.bfloat16))


FIRST = 80
BATCH = 4


def layer_kernel(
    length_ref,
    resid_ref,
    query_ref,
    key_ref,
    value_ref,
    gain_ref,
    slots_ref,
    router_ref,
    cache_hbm,
    project_hbm,
    gate_up_hbm,
    down_hbm,
    after_ref,
    out_ref,
    cache,
    project,
    attended,
    share_out,
    share_in,
    squares_out,
    squares_in,
    logits_out,
    logits_in,
    tables,
    tokens,
    partial,
    from_core,
    from_x,
    from_x_last,
    from_y,
    from_y_last,
    from_z,
    from_z_last,
    gate_up,
    down,
    rows_in,
    hidden,
    combine,
    weight_sem,
    send_sem,
    recv_sem,
):
    count, width = resid_ref.shape
    capacity = combine.shape[1]
    experts = router_ref.shape[0]
    here = lax.axis_index("grp")
    there = 1 - here
    place = lax.axis_index("ep")
    core = lax.rem(place, 2)
    y_at = lax.rem(lax.div(place, 2), 2)
    z_low = lax.rem(lax.div(place, 4), 2)
    z_high = lax.div(place, 8)

    def moved(dz, dy, dc):
        high = 1 - z_high if dz // 2 else z_high
        low = 1 - z_low if dz % 2 else z_low
        along_y = 1 - y_at if dy else y_at
        on_core = 1 - core if dc else core
        return ((high * 2 + low) * 2 + along_y) * 2 + on_core

    by_x = (there, place)
    by_y = (here, moved(0, 1, 0))
    by_core = (here, moved(0, 0, 1))
    by_z = [None] + [(here, moved(dz, 0, 0)) for dz in (1, 2, 3)]

    keys = pltpu.make_async_copy(cache_hbm.at[0], cache.at[0], weight_sem.at[0])
    values = pltpu.make_async_copy(cache_hbm.at[1], cache.at[1], weight_sem.at[1])
    projection = [
        pltpu.make_async_copy(
            project_hbm.at[:, half * width : (half + 1) * width],
            project.at[half],
            weight_sem.at[2 + half],
        )
        for half in (0, 1)
    ]
    weights = [
        pltpu.make_async_copy(gate_up_hbm.at[0], gate_up, weight_sem.at[4]),
        pltpu.make_async_copy(down_hbm.at[0], down, weight_sem.at[5]),
    ]
    for one in [keys, values] + projection + weights:
        one.start()

    barrier = pltpu.get_barrier_semaphore()
    peers = [by_x, by_y, by_core] + by_z[1:]
    for peer in peers:
        pl.semaphore_signal(barrier, inc=1, device_id=peer, device_id_type=pl.DeviceIdType.MESH)

    tables[0, 0] = slots_ref[...]
    pl.semaphore_wait(barrier, len(peers))

    first = pl.ds(0, FIRST)
    last = pl.ds(FIRST, count - FIRST)
    started = []

    def send(source, target, peer):
        index = len(started)
        copy = pltpu.make_async_remote_copy(
            src_ref=source,
            dst_ref=target,
            send_sem=send_sem.at[index],
            recv_sem=recv_sem.at[index],
            device_id=peer,
            device_id_type=pl.DeviceIdType.MESH,
        )
        copy.start()
        started.append(copy)
        return copy

    def gather_x(slot):
        piece = tokens.at[slot, here, first]
        return send(piece, piece, by_x)

    def gather_y(dz):
        return send(tokens.at[dz, here, first], tokens.at[4 + dz, here, first], by_y)

    def gather_y_last(dz):
        return send(tokens.at[dz, :, last], tokens.at[4 + dz, :, last], by_y)

    def gather_core(slot):
        return send(tokens.at[slot], tokens.at[8 + slot], by_core)

    score_scale = float(HD) ** (-0.5)
    live_rows = (
        lax.broadcasted_iota(jnp.int32, (count, cache.shape[1]), 1) < length_ref[place]
    )
    causal = lax.broadcasted_iota(jnp.int32, (count, count), 0) >= lax.broadcasted_iota(
        jnp.int32, (count, count), 1
    )
    along_last = (((1,), (1,)), ((), ()))
    keys.wait()
    values.wait()
    for start in range(0, width, HD):
        columns = slice(start, start + HD)
        asked = query_ref[:, columns]
        new_scores = score_scale * lax.dot_general(
            asked, key_ref[:, columns], along_last, preferred_element_type=jnp.float32
        )
        old_scores = score_scale * lax.dot_general(
            asked, cache[0, :, columns], along_last, preferred_element_type=jnp.float32
        )
        new_scores = jnp.where(causal, new_scores, MASKED)
        old_scores = jnp.where(live_rows, old_scores, MASKED)
        row_max = jnp.maximum(
            jnp.max(new_scores, axis=1, keepdims=True), jnp.max(old_scores, axis=1, keepdims=True)
        )
        new_probs = jnp.exp(new_scores - row_max)
        old_probs = jnp.exp(old_scores - row_max)
        denominator = jnp.sum(new_probs, axis=1, keepdims=True) + jnp.sum(
            old_probs, axis=1, keepdims=True
        )
        weighted = jnp.dot(
            new_probs.astype(jnp.bfloat16),
            value_ref[:, columns],
            preferred_element_type=jnp.float32,
        ) + jnp.dot(
            old_probs.astype(jnp.bfloat16),
            cache[1, :, columns],
            preferred_element_type=jnp.float32,
        )
        attended[:, columns] = (weighted / denominator).astype(jnp.bfloat16)

    for one in projection:
        one.wait()
    share_out[...] = jnp.dot(
        attended[...], project[there], preferred_element_type=jnp.float32
    ).astype(jnp.bfloat16)
    share = send(share_out, share_in, by_x)
    own_share = jnp.dot(attended[...], project[here], preferred_element_type=jnp.float32)
    share.wait_recv()
    after = (
        resid_ref[...].astype(jnp.float32) + (own_share + share_in[...].astype(jnp.float32))
    ).astype(jnp.bfloat16)
    after_ref[...] = after
    after = after.astype(jnp.float32)
    squares = jnp.sum(after * after, axis=1, keepdims=True)
    squares_out[...] = jnp.transpose(jnp.broadcast_to(squares, (count, 128)))[:8]
    squares_sent = send(squares_out, squares_in, by_x)
    squares_sent.wait_recv()
    squares = squares + jnp.transpose(jnp.broadcast_to(squares_in[:1], (128, count)))[:, :1]
    inverse = lax.rsqrt(squares / (2 * width) + EPS)
    half_here = pl.ds(pl.multiple_of(here * width, 128), width)
    normed = (after * inverse * gain_ref[:, half_here]).astype(jnp.bfloat16)
    tokens[0, here] = normed

    own_logits = lax.dot_general(
        router_ref[:, half_here], normed, along_last, preferred_element_type=jnp.float32
    )
    logits_out[...] = own_logits
    logits_sent = send(logits_out, logits_in, by_x)
    x_last = send(tokens.at[0, here, last], tokens.at[0, here, last], by_x)
    y_first = {0: gather_y(0)}
    x_first = {0: gather_x(0)}
    z_first = {}
    z_last = {}
    y_last = {}
    to_core = {}

    def gather_z(dz):
        z_first[dz] = send(tokens.at[0, here, first], tokens.at[dz, here, first], by_z[dz])

    def gather_z_last(dz):
        z_last[dz] = send(tokens.at[0, :, last], tokens.at[dz, :, last], by_z[dz])

    gather_z(1)
    logits_sent.wait_recv()
    logits = jnp.where(slots_ref[...] >= 0.0, own_logits + logits_in[...], MASKED)
    raised = jnp.exp(logits - jnp.max(logits, axis=0, keepdims=True))
    tables[0, 1] = raised / jnp.sum(raised, axis=0, keepdims=True)
    table_z = {dz: send(tables.at[0], tables.at[dz], by_z[dz]) for dz in (1, 2, 3)}
    table_y = {0: send(tables.at[0], tables.at[4], by_y)}
    table_core = {0: send(tables.at[0], tables.at[8], by_core)}
    x_last.wait_recv()
    gather_z_last(1)
    y_last[0] = gather_y_last(0)
    gather_z(3)
    gather_z_last(3)

    def pass_first():
        z_first[3].wait_recv()
        z_first[2] = send(tokens.at[3, here, first], tokens.at[2, here, first], by_z[1])
        y_first[3] = gather_y(3)
        x_first[3] = gather_x(3)

    def pass_last():
        z_last[3].wait_recv()
        z_last[2] = send(tokens.at[3, :, last], tokens.at[2, :, last], by_z[1])
        y_last[3] = gather_y_last(3)

    def pass_tables():
        for dz in (1, 2, 3):
            table_z[dz].wait_recv()
            table_y[dz] = send(tables.at[dz], tables.at[4 + dz], by_y)
            table_core[dz] = send(tables.at[dz], tables.at[8 + dz], by_core)

    def arrive_z(dz):
        z_first[dz].wait_recv()
        y_first[dz] = gather_y(dz)
        x_first[dz] = gather_x(dz)
        z_last[dz].wait_recv()
        y_last[dz] = gather_y_last(dz)

    def arrive_y(dz):
        table_y[dz].wait_recv()
        table_core[4 + dz] = send(tables.at[4 + dz], tables.at[12 + dz], by_core)
        y_first[dz].wait_recv()
        x_first[4 + dz] = gather_x(4 + dz)
        x_first[dz].wait_recv()
        to_core[dz] = gather_core(dz)

    def arrive_x(dz):
        x_first[4 + dz].wait_recv()
        y_last[dz].wait_recv()
        to_core[4 + dz] = gather_core(4 + dz)

    expert_row = lax.broadcasted_iota(jnp.int32, (experts, count), 0) == place
    slot_row = lax.broadcasted_iota(jnp.int32, (capacity, count), 0)
    units = hidden.shape[1]
    features = rows_in.shape[1]

    def rows_of(step):
        return slice(step * capacity, (step + 1) * capacity)

    def hidden_on(dz):
        for step in range(BATCH):
            slot = dz + 4 * step
            mine, weight = (
                jnp.sum(jnp.where(expert_row, tables[slot, part], 0.0), axis=0, keepdims=True)
                for part in (0, 1)
            )
            chosen = slot_row == mine.astype(jnp.int32)
            combine[step] = jnp.where(chosen, weight, 0.0).astype(jnp.bfloat16)
            select = jnp.where(chosen, 1.0, 0.0).astype(jnp.bfloat16)
            for half in (0, 1):
                rows_in[rows_of(step), half * width : (half + 1) * width] = jnp.dot(
                    select, tokens[slot, half], preferred_element_type=jnp.float32
                ).astype(jnp.bfloat16)
        for start in range(0, units, 256):
            stop = min(start + 256, units)
            gate_value, up_value = (
                lax.dot_general(
                    rows_in[...],
                    gate_up[part, start:stop],
                    along_last,
                    preferred_element_type=jnp.float32,
                )
                for part in (0, 1)
            )
            hidden[:, start:stop] = (gate_value / (1.0 + jnp.exp(-gate_value)) * up_value).astype(
                jnp.bfloat16
            )

    def answers_on(dz):
        for start in range(0, features, 512):
            stop = min(start + 512, features)
            rows_in[:, start:stop] = jnp.dot(
                hidden[...], down[:, start:stop], preferred_element_type=jnp.float32
            ).astype(jnp.bfloat16)
        for step in (3, 2, 1, 0):
            slot = dz + 4 * step
            for half in (0, 1):
                partial[slot, half] = lax.dot_general(
                    combine[step],
                    rows_in[rows_of(step), half * width : (half + 1) * width],
                    (((0,), (0,)), ((), ())),
                    preferred_element_type=jnp.float32,
                ).astype(jnp.bfloat16)
            if slot >= 8:
                back_core[slot - 8] = return_core(slot - 8)

    def added(one, other):
        return one + other

    def return_core(slot):
        return send(partial.at[8 + slot], from_core.at[slot], by_core)

    def return_x(slot):
        return send(partial.at[slot, there, first], from_x.at[slot], by_x)

    back_core = {}
    back_x = {}
    back_y = {}
    back_y_last = {}
    back_z = {}
    back_z_last = {}

    def answer_rows(dz):
        for slot in (dz, 4 + dz):
            table_core[slot].wait_recv()
            to_core[slot].wait_recv()
        hidden_on(dz)

    def core_sum(dz):
        for slot in (4 + dz, dz):
            back_core[slot].wait_recv()
            partial[slot] = added(partial[slot], from_core[slot])
            back_x[slot] = return_x(slot)
            if slot >= 4:
                back_y_last[dz] = send(partial.at[slot, :, last], from_y_last.at[dz], by_y)

    def x_sum(dz):
        back_x[4 + dz].wait_recv()
        partial[4 + dz, here, :FIRST] = added(partial[4 + dz, here, :FIRST], from_x[4 + dz])
        back_y[dz] = send(partial.at[4 + dz, here, first], from_y.at[dz], by_y)

    def y_sum(dz):
        back_y_last[dz].wait_recv()
        total = added(partial[dz, :, FIRST:], from_y_last[dz])
        if dz == 2:
            back_z_last[3].wait_recv()
            total = added(total, from_z_last[2])
        partial[dz, :, FIRST:] = total
        back_z_last[dz] = send(
            partial.at[dz, :, last], from_z_last.at[dz - 1], by_z[2 if dz == 2 else 1]
        )
        back_x[dz].wait_recv()
        back_y[dz].wait_recv()
        total = (
            partial[dz, here, :FIRST].astype(jnp.float32)
            + from_x[dz].astype(jnp.float32)
            + from_y[dz].astype(jnp.float32)
        )
        if dz == 2:
            back_z[3].wait_recv()
            total = total + from_z[2].astype(jnp.float32)
        partial[dz, here, :FIRST] = total.astype(jnp.bfloat16)
        back_z[dz] = send(
            partial.at[dz, here, first], from_z.at[dz - 1], by_z[2 if dz == 2 else 1]
        )

    arrive_y(0)
    arrive_z(1)
    pass_tables()
    arrive_x(0)
    arrive_y(1)
    for one in weights:
        one.wait()
    answer_rows(0)
    pass_first()
    answers_on(0)
    arrive_x(1)
    core_sum(0)
    answer_rows(1)
    pass_last()
    answers_on(1)
    arrive_y(3)
    arrive_z(2)
    x_sum(0)
    arrive_x(3)
    core_sum(1)
    arrive_y(2)
    answer_rows(3)
    answers_on(3)
    arrive_x(2)
    x_sum(1)
    answer_rows(2)
    core_sum(3)
    answers_on(2)
    y_sum(1)
    x_sum(3)
    core_sum(2)
    y_sum(3)
    x_sum(2)
    y_sum(2)
    back_y_last[0].wait_recv()
    for dz in (1, 2):
        back_z_last[dz].wait_recv()

    def last_sum(half):
        total = partial[0, half, FIRST:].astype(jnp.float32) + from_y_last[0, half].astype(
            jnp.float32
        )
        for dz in (1, 2):
            total = total + from_z_last[dz - 1, half].astype(jnp.float32)
        return total

    partial[0, there, FIRST:] = last_sum(there).astype(jnp.bfloat16)
    back_x_last = send(partial.at[0, there, last], from_x_last, by_x)
    back_x[0].wait_recv()
    back_y[0].wait_recv()
    for dz in (1, 2):
        back_z[dz].wait_recv()
    total = (
        partial[0, here, :FIRST].astype(jnp.float32)
        + from_x[0].astype(jnp.float32)
        + from_y[0].astype(jnp.float32)
    )
    for dz in (1, 2):
        total = total + from_z[dz - 1].astype(jnp.float32)
    out_ref[:FIRST] = total.astype(jnp.bfloat16)
    total = last_sum(here)
    back_x_last.wait_recv()
    out_ref[FIRST:] = (total + from_x_last[...].astype(jnp.float32)).astype(jnp.bfloat16)
    for copy in started:
        copy.wait_send()


def layer(
    lengths,
    resid,
    query,
    key_new,
    value_new,
    gain,
    slots,
    router_rows,
    cache_kv,
    w_out,
    gate_up_rows,
    w_down,
    capacity,
):
    count, width = resid.shape
    units = w_down.shape[1]
    rest = count - FIRST
    low = jnp.bfloat16
    wide = jnp.float32
    vmem = pl.BlockSpec(memory_space=pltpu.VMEM)
    hbm = pl.BlockSpec(memory_space=pl.ANY)
    block = jax.ShapeDtypeStruct((count, width), low)
    return pl.pallas_call(
        layer_kernel,
        out_shape=(block, block),
        in_specs=[pl.BlockSpec(memory_space=pltpu.SMEM)] + [vmem] * 7 + [hbm] * 4,
        out_specs=(vmem, vmem),
        scratch_shapes=[
            pltpu.VMEM(cache_kv.shape, low),
            pltpu.VMEM((2, width, width), low),
            pltpu.VMEM((count, width), low),
            pltpu.VMEM((count, width), low),
            pltpu.VMEM((count, width), low),
            pltpu.VMEM((8, count), wide),
            pltpu.VMEM((8, count), wide),
            pltpu.VMEM(slots.shape, wide),
            pltpu.VMEM(slots.shape, wide),
            pltpu.VMEM((16, 2) + slots.shape, wide),
            pltpu.VMEM((16, 2, count, width), low),
            pltpu.VMEM((16, 2, count, width), low),
            pltpu.VMEM((8, 2, count, width), low),
            pltpu.VMEM((8, FIRST, width), low),
            pltpu.VMEM((rest, width), low),
            pltpu.VMEM((4, FIRST, width), low),
            pltpu.VMEM((4, 2, rest, width), low),
            pltpu.VMEM((3, FIRST, width), low),
            pltpu.VMEM((3, 2, rest, width), low),
            pltpu.VMEM((2, units, 2 * width), low),
            pltpu.VMEM((units, 2 * width), low),
            pltpu.VMEM((BATCH * capacity, 2 * width), low),
            pltpu.VMEM((BATCH * capacity, units), low),
            pltpu.VMEM((BATCH, capacity, count), low),
            pltpu.SemaphoreType.DMA((6,)),
            pltpu.SemaphoreType.DMA((80,)),
            pltpu.SemaphoreType.DMA((80,)),
        ],
        compiler_params=pltpu.CompilerParams(
            collective_id=0, has_side_effects=True, vmem_limit_bytes=60 * 1024 * 1024
        ),
        cost_estimate=pl.CostEstimate(
            flops=12_000_000_000, bytes_accessed=18_000_000, transcendentals=2_000_000
        ),
    )(
        lengths,
        resid,
        query,
        key_new,
        value_new,
        gain,
        slots,
        router_rows,
        cache_kv,
        w_out,
        gate_up_rows,
        w_down,
    )


def slot_table(routes, experts_all):
    tokens_here = routes.shape[0]
    hits = jnp.any(
        routes.T[None, :, :] == jnp.arange(experts_all, dtype=jnp.int32)[:, None, None], axis=1
    )
    position = jnp.arange(tokens_here, dtype=jnp.int32)
    earlier = (position[:, None] < position[None, :]).astype(jnp.bfloat16)
    slots = jnp.dot(hits.astype(jnp.bfloat16), earlier, preferred_element_type=jnp.float32)
    return jnp.where(hits, slots, -1.0)


def routed_body(
    resid,
    query,
    key_new,
    value_new,
    cache_kv,
    cache_len,
    w_out,
    norm_gain,
    w_router,
    routes,
    w_gate_up,
    w_down,
):
    experts_all = w_router.shape[1]
    width = resid.shape[1]
    capacity = max(2, 8 * resid.shape[0] // lax.axis_size("ep"))
    return layer(
        cache_len,
        resid,
        query,
        key_new,
        value_new,
        norm_gain.astype(jnp.float32).reshape(1, 2 * width),
        slot_table(routes, experts_all),
        w_router.T,
        cache_kv,
        w_out,
        jnp.swapaxes(w_gate_up, 2, 3),
        w_down,
        capacity,
    )


def solution(mesh):
    fits = mesh.shape["ep"] == 16 and mesh.shape["grp"] == 2
    return jax.shard_map(
        routed_body if fits else wide_body,
        mesh=mesh,
        in_specs=(
            P("ep", "grp"),
            P("ep", "grp"),
            P("ep", "grp"),
            P("ep", "grp"),
            P(None, "ep", "grp"),
            P(),
            P("grp", None),
            P(),
            P(),
            P("ep", None),
            P("ep", None, None, "grp"),
            P("ep", "grp", None),
        ),
        out_specs=(P("ep", "grp"), P("ep", "grp")),
        check_vma=False,
    )
```

```python
import jax
import jax.numpy as jnp
from jax import lax
from jax.experimental import pallas as pl
from jax.experimental.pallas import tpu as pltpu
from jax.sharding import PartitionSpec as P

D = 2048
HD = 128
TOP = 4


EPS = 1e-06
MASKED = -1e30


def expert_rows(arrived, w_gate_up, w_down):
    features = arrived.shape[-1]
    flat_rows = arrived.reshape(-1, features)
    gate_value = jnp.dot(flat_rows, w_gate_up[0, 0], preferred_element_type=jnp.float32)
    up_value = jnp.dot(flat_rows, w_gate_up[0, 1], preferred_element_type=jnp.float32)
    hidden = (jax.nn.silu(gate_value) * up_value).astype(jnp.bfloat16)
    partial_value = jnp.dot(hidden, w_down[0], preferred_element_type=jnp.float32).astype(
        jnp.bfloat16
    )
    return partial_value.reshape(arrived.shape)


def send_back(answered):
    return lax.all_to_all(answered, "ep", split_axis=0, concat_axis=0, tiled=True)


def wide_body(
    resid,
    query,
    key_new,
    value_new,
    cache_kv,
    cache_len,
    w_out,
    norm_gain,
    w_router,
    routes,
    w_gate_up,
    w_down,
):
    tokens_here = query.shape[0]
    heads_here = query.shape[1] // HD
    experts_all = w_router.shape[1]
    column_width = resid.shape[1]
    group_index = lax.axis_index("grp")
    request = lax.axis_index("ep")
    capacity = max(2, 8 * tokens_here // lax.axis_size("ep"))
    score_scale = float(HD) ** (-0.5)
    column_start = group_index * column_width
    queries = query.reshape(tokens_here, heads_here, HD)
    new_keys = key_new.reshape(tokens_here, heads_here, HD)
    new_values = value_new.reshape(tokens_here, heads_here, HD)
    cache_rows = cache_kv.shape[1]
    cache_keys = cache_kv[0].reshape(cache_rows, heads_here, HD)
    cache_values = cache_kv[1].reshape(cache_rows, heads_here, HD)
    own_length = lax.dynamic_index_in_dim(cache_len, request, 0, keepdims=False)
    position = jnp.arange(tokens_here, dtype=jnp.int32)
    causal = (position[:, None] >= position[None, :])[:, None, :]
    new_scores = (
        jnp.einsum("qhd,khd->qhk", queries, new_keys, preferred_element_type=jnp.float32)
        * score_scale
    )
    new_scores = jnp.where(causal, new_scores, MASKED)
    live_rows = (jnp.arange(cache_rows, dtype=jnp.int32) < own_length)[None, None, :]
    old_scores = (
        jnp.einsum("qhd,khd->qhk", queries, cache_keys, preferred_element_type=jnp.float32)
        * score_scale
    )
    old_scores = jnp.where(live_rows, old_scores, MASKED)
    row_max = jnp.maximum(jnp.max(new_scores, axis=-1), jnp.max(old_scores, axis=-1))
    new_probs = jnp.exp(new_scores - row_max[..., None])
    old_probs = jnp.exp(old_scores - row_max[..., None])
    denominator = jnp.sum(new_probs, axis=-1) + jnp.sum(old_probs, axis=-1)
    weighted = jnp.einsum(
        "qhk,khd->qhd",
        new_probs.astype(jnp.bfloat16),
        new_values,
        preferred_element_type=jnp.float32,
    )
    weighted = weighted + jnp.einsum(
        "qhk,khd->qhd",
        old_probs.astype(jnp.bfloat16),
        cache_values,
        preferred_element_type=jnp.float32,
    )
    attended = (
        (weighted / denominator[..., None])
        .astype(jnp.bfloat16)
        .reshape(tokens_here, heads_here * HD)
    )
    projected = jnp.dot(attended, w_out, preferred_element_type=jnp.float32)
    attn_share = lax.psum_scatter(projected, "grp", scatter_dimension=1, tiled=True)
    after_cols = (resid.astype(jnp.float32) + attn_share).astype(jnp.bfloat16)
    after_wide = after_cols.astype(jnp.float32)
    squares = lax.psum(jnp.sum(after_wide * after_wide, axis=1), "grp")
    inverse = lax.rsqrt(squares / D + EPS)
    gain_cols = lax.dynamic_slice_in_dim(norm_gain, column_start, column_width, 0)
    normed_cols = (after_wide * inverse[:, None] * gain_cols.astype(jnp.float32)[None, :]).astype(
        jnp.bfloat16
    )
    router_cols = lax.dynamic_slice_in_dim(w_router, column_start, column_width, 0)
    logits = lax.psum(jnp.dot(normed_cols, router_cols, preferred_element_type=jnp.float32), "grp")
    normed_full = lax.all_gather(normed_cols, "grp", axis=1, tiled=True)
    route_hits = routes[:, :, None] == jnp.arange(experts_all, dtype=jnp.int32)[None, None, :]
    chosen = jnp.sum(jnp.where(route_hits, logits[:, None, :], 0.0), axis=-1)
    route_weight = jax.nn.softmax(chosen, axis=-1).astype(jnp.bfloat16)
    flat_hits = route_hits.reshape(tokens_here * TOP, experts_all).astype(jnp.int32)
    earlier = jnp.cumsum(flat_hits, axis=0) - flat_hits
    slot_index = jnp.sum(earlier * flat_hits, axis=1)
    slot_row = (routes.reshape(-1) * capacity + slot_index).reshape(tokens_here, TOP)
    slot_ids = jnp.arange(experts_all * capacity, dtype=jnp.int32)
    matches = slot_row[:, :, None] == slot_ids[None, None, :]
    selection = jnp.any(matches, axis=1).astype(jnp.bfloat16)
    combine = jnp.sum(
        jnp.where(matches, route_weight[:, :, None], jnp.zeros((), jnp.bfloat16)), axis=1
    )
    outgoing = jnp.einsum(
        "tj,td->jd", selection, normed_full, preferred_element_type=jnp.float32
    ).astype(jnp.bfloat16)
    outgoing = outgoing.reshape(experts_all, capacity, D)
    returned = send_back(
        expert_rows(
            lax.all_to_all(outgoing, "ep", split_axis=0, concat_axis=0, tiled=True),
            w_gate_up,
            w_down,
        )
    )
    mixed_part = jnp.dot(
        combine, returned.reshape(experts_all * capacity, D), preferred_element_type=jnp.float32
    )
    mixed_cols = lax.psum_scatter(mixed_part, "grp", scatter_dimension=1, tiled=True)
    return (after_cols, mixed_cols.astype(jnp.bfloat16))


FIRST = 80
BATCH = 4


def layer_kernel(
    length_ref,
    resid_ref,
    query_ref,
    key_ref,
    value_ref,
    gain_ref,
    slots_ref,
    router_ref,
    cache_hbm,
    project_hbm,
    gate_up_hbm,
    down_hbm,
    after_ref,
    out_ref,
    cache,
    project,
    attended,
    share_out,
    share_in,
    squares_out,
    squares_in,
    logits_out,
    logits_in,
    tables,
    tokens,
    partial,
    from_core,
    from_x,
    from_x_last,
    from_y,
    from_y_last,
    from_z,
    from_z_last,
    gate_up,
    down,
    rows_in,
    hidden,
    combine,
    weight_sem,
    send_sem,
    recv_sem,
):
    count, width = resid_ref.shape
    capacity = combine.shape[1]
    experts = router_ref.shape[0]
    here = lax.axis_index("grp")
    there = 1 - here
    place = lax.axis_index("ep")
    core = lax.rem(place, 2)
    y_at = lax.rem(lax.div(place, 2), 2)
    z_low = lax.rem(lax.div(place, 4), 2)
    z_high = lax.div(place, 8)

    def moved(dz, dy, dc):
        high = 1 - z_high if dz // 2 else z_high
        low = 1 - z_low if dz % 2 else z_low
        along_y = 1 - y_at if dy else y_at
        on_core = 1 - core if dc else core
        return ((high * 2 + low) * 2 + along_y) * 2 + on_core

    by_x = (there, place)
    by_y = (here, moved(0, 1, 0))
    by_core = (here, moved(0, 0, 1))
    by_z = [None] + [(here, moved(dz, 0, 0)) for dz in (1, 2, 3)]

    keys = pltpu.make_async_copy(cache_hbm.at[0], cache.at[0], weight_sem.at[0])
    values = pltpu.make_async_copy(cache_hbm.at[1], cache.at[1], weight_sem.at[1])
    projection = [
        pltpu.make_async_copy(
            project_hbm.at[:, half * width : (half + 1) * width],
            project.at[half],
            weight_sem.at[2 + half],
        )
        for half in (0, 1)
    ]
    weights = [
        pltpu.make_async_copy(gate_up_hbm.at[0], gate_up, weight_sem.at[4]),
        pltpu.make_async_copy(down_hbm.at[0], down, weight_sem.at[5]),
    ]
    for one in [keys, values] + projection + weights:
        one.start()

    barrier = pltpu.get_barrier_semaphore()
    peers = [by_x, by_y, by_core] + by_z[1:]
    for peer in peers:
        pl.semaphore_signal(barrier, inc=1, device_id=peer, device_id_type=pl.DeviceIdType.MESH)

    tables[0, 0] = slots_ref[...]
    pl.semaphore_wait(barrier, len(peers))

    first = pl.ds(0, FIRST)
    last = pl.ds(FIRST, count - FIRST)
    started = []

    def send(source, target, peer):
        index = len(started)
        copy = pltpu.make_async_remote_copy(
            src_ref=source,
            dst_ref=target,
            send_sem=send_sem.at[index],
            recv_sem=recv_sem.at[index],
            device_id=peer,
            device_id_type=pl.DeviceIdType.MESH,
        )
        copy.start()
        started.append(copy)
        return copy

    def gather_x(slot):
        piece = tokens.at[slot, here, first]
        return send(piece, piece, by_x)

    def gather_y(dz):
        return send(tokens.at[dz, here, first], tokens.at[4 + dz, here, first], by_y)

    def gather_y_last(dz):
        return send(tokens.at[dz, :, last], tokens.at[4 + dz, :, last], by_y)

    def gather_core(slot):
        return send(tokens.at[slot], tokens.at[8 + slot], by_core)

    score_scale = float(HD) ** (-0.5)
    live_rows = (
        lax.broadcasted_iota(jnp.int32, (count, cache.shape[1]), 1) < length_ref[place]
    )
    causal = lax.broadcasted_iota(jnp.int32, (count, count), 0) >= lax.broadcasted_iota(
        jnp.int32, (count, count), 1
    )
    along_last = (((1,), (1,)), ((), ()))
    keys.wait()
    values.wait()
    for start in range(0, width, HD):
        columns = slice(start, start + HD)
        asked = query_ref[:, columns]
        new_scores = score_scale * lax.dot_general(
            asked, key_ref[:, columns], along_last, preferred_element_type=jnp.float32
        )
        old_scores = score_scale * lax.dot_general(
            asked, cache[0, :, columns], along_last, preferred_element_type=jnp.float32
        )
        new_scores = jnp.where(causal, new_scores, MASKED)
        old_scores = jnp.where(live_rows, old_scores, MASKED)
        row_max = jnp.maximum(
            jnp.max(new_scores, axis=1, keepdims=True), jnp.max(old_scores, axis=1, keepdims=True)
        )
        new_probs = jnp.exp(new_scores - row_max)
        old_probs = jnp.exp(old_scores - row_max)
        denominator = jnp.sum(new_probs, axis=1, keepdims=True) + jnp.sum(
            old_probs, axis=1, keepdims=True
        )
        weighted = jnp.dot(
            new_probs.astype(jnp.bfloat16),
            value_ref[:, columns],
            preferred_element_type=jnp.float32,
        ) + jnp.dot(
            old_probs.astype(jnp.bfloat16),
            cache[1, :, columns],
            preferred_element_type=jnp.float32,
        )
        attended[:, columns] = (weighted / denominator).astype(jnp.bfloat16)

    for one in projection:
        one.wait()
    share_out[...] = jnp.dot(
        attended[...], project[there], preferred_element_type=jnp.float32
    ).astype(jnp.bfloat16)
    share = send(share_out, share_in, by_x)
    own_share = jnp.dot(attended[...], project[here], preferred_element_type=jnp.float32)
    share.wait_recv()
    after = (
        resid_ref[...].astype(jnp.float32) + (own_share + share_in[...].astype(jnp.float32))
    ).astype(jnp.bfloat16)
    after_ref[...] = after
    after = after.astype(jnp.float32)
    squares = jnp.sum(after * after, axis=1, keepdims=True)
    squares_out[...] = jnp.transpose(jnp.broadcast_to(squares, (count, 128)))[:8]
    squares_sent = send(squares_out, squares_in, by_x)
    squares_sent.wait_recv()
    squares = squares + jnp.transpose(jnp.broadcast_to(squares_in[:1], (128, count)))[:, :1]
    inverse = lax.rsqrt(squares / (2 * width) + EPS)
    half_here = pl.ds(pl.multiple_of(here * width, 128), width)
    normed = (after * inverse * gain_ref[:, half_here]).astype(jnp.bfloat16)
    tokens[0, here] = normed

    own_logits = lax.dot_general(
        router_ref[:, half_here], normed, along_last, preferred_element_type=jnp.float32
    )
    logits_out[...] = own_logits
    logits_sent = send(logits_out, logits_in, by_x)
    x_last = send(tokens.at[0, here, last], tokens.at[0, here, last], by_x)
    y_first = {0: gather_y(0)}
    x_first = {0: gather_x(0)}
    z_first = {}
    z_last = {}
    y_last = {}
    to_core = {}

    def gather_z(dz):
        z_first[dz] = send(tokens.at[0, here, first], tokens.at[dz, here, first], by_z[dz])

    def gather_z_last(dz):
        z_last[dz] = send(tokens.at[0, :, last], tokens.at[dz, :, last], by_z[dz])

    gather_z(1)
    logits_sent.wait_recv()
    logits = jnp.where(slots_ref[...] >= 0.0, own_logits + logits_in[...], MASKED)
    raised = jnp.exp(logits - jnp.max(logits, axis=0, keepdims=True))
    tables[0, 1] = raised / jnp.sum(raised, axis=0, keepdims=True)
    table_z = {dz: send(tables.at[0], tables.at[dz], by_z[dz]) for dz in (1, 2, 3)}
    table_y = {0: send(tables.at[0], tables.at[4], by_y)}
    table_core = {0: send(tables.at[0], tables.at[8], by_core)}
    x_last.wait_recv()
    gather_z_last(1)
    y_last[0] = gather_y_last(0)
    gather_z(3)
    gather_z_last(3)

    def pass_first():
        z_first[3].wait_recv()
        z_first[2] = send(tokens.at[3, here, first], tokens.at[2, here, first], by_z[1])
        y_first[3] = gather_y(3)
        x_first[3] = gather_x(3)

    def pass_last():
        z_last[3].wait_recv()
        z_last[2] = send(tokens.at[3, :, last], tokens.at[2, :, last], by_z[1])
        y_last[3] = gather_y_last(3)

    def pass_tables():
        for dz in (1, 2, 3):
            table_z[dz].wait_recv()
            table_y[dz] = send(tables.at[dz], tables.at[4 + dz], by_y)
            table_core[dz] = send(tables.at[dz], tables.at[8 + dz], by_core)

    def arrive_z(dz):
        z_first[dz].wait_recv()
        y_first[dz] = gather_y(dz)
        x_first[dz] = gather_x(dz)
        z_last[dz].wait_recv()
        y_last[dz] = gather_y_last(dz)

    def arrive_y(dz):
        table_y[dz].wait_recv()
        table_core[4 + dz] = send(tables.at[4 + dz], tables.at[12 + dz], by_core)
        y_first[dz].wait_recv()
        x_first[4 + dz] = gather_x(4 + dz)
        x_first[dz].wait_recv()
        to_core[dz] = gather_core(dz)

    def arrive_x(dz):
        x_first[4 + dz].wait_recv()
        y_last[dz].wait_recv()
        to_core[4 + dz] = gather_core(4 + dz)

    expert_row = lax.broadcasted_iota(jnp.int32, (experts, count), 0) == place
    slot_row = lax.broadcasted_iota(jnp.int32, (capacity, count), 0)
    units = hidden.shape[1]
    features = rows_in.shape[1]

    def rows_of(step):
        return slice(step * capacity, (step + 1) * capacity)

    def hidden_on(dz):
        for step in range(BATCH):
            slot = dz + 4 * step
            mine, weight = (
                jnp.sum(jnp.where(expert_row, tables[slot, part], 0.0), axis=0, keepdims=True)
                for part in (0, 1)
            )
            chosen = slot_row == mine.astype(jnp.int32)
            combine[step] = jnp.where(chosen, weight, 0.0).astype(jnp.bfloat16)
            select = jnp.where(chosen, 1.0, 0.0).astype(jnp.bfloat16)
            for half in (0, 1):
                rows_in[rows_of(step), half * width : (half + 1) * width] = jnp.dot(
                    select, tokens[slot, half], preferred_element_type=jnp.float32
                ).astype(jnp.bfloat16)
        gate_value, up_value = (
            lax.dot_general(
                gate_up[part], rows_in[...], along_last, preferred_element_type=jnp.float32
            )
            for part in (0, 1)
        )
        hidden[...] = jnp.transpose(
            (gate_value / (1.0 + jnp.exp(-gate_value)) * up_value).astype(jnp.bfloat16)
        )

    def answers_on(dz):
        for start in range(0, features, 512):
            stop = min(start + 512, features)
            rows_in[:, start:stop] = jnp.dot(
                hidden[...], down[:, start:stop], preferred_element_type=jnp.float32
            ).astype(jnp.bfloat16)
        for step in (3, 2, 1, 0):
            slot = dz + 4 * step
            for half in (0, 1):
                partial[slot, half] = lax.dot_general(
                    combine[step],
                    rows_in[rows_of(step), half * width : (half + 1) * width],
                    (((0,), (0,)), ((), ())),
                    preferred_element_type=jnp.float32,
                ).astype(jnp.bfloat16)
            if slot >= 8:
                back_core[slot - 8] = return_core(slot - 8)

    def added(one, other):
        return one + other

    def return_core(slot):
        return send(partial.at[8 + slot], from_core.at[slot], by_core)

    def return_x(slot):
        return send(partial.at[slot, there, first], from_x.at[slot], by_x)

    back_core = {}
    back_x = {}
    back_y = {}
    back_y_last = {}
    back_z = {}
    back_z_last = {}

    def answer_rows(dz):
        for slot in (dz, 4 + dz):
            table_core[slot].wait_recv()
            to_core[slot].wait_recv()
        hidden_on(dz)

    def core_sum(dz):
        for slot in (4 + dz, dz):
            back_core[slot].wait_recv()
            partial[slot] = added(partial[slot], from_core[slot])
            back_x[slot] = return_x(slot)
            if slot >= 4:
                back_y_last[dz] = send(partial.at[slot, :, last], from_y_last.at[dz], by_y)

    def x_sum(dz):
        back_x[4 + dz].wait_recv()
        partial[4 + dz, here, :FIRST] = added(partial[4 + dz, here, :FIRST], from_x[4 + dz])
        back_y[dz] = send(partial.at[4 + dz, here, first], from_y.at[dz], by_y)

    def y_sum(dz):
        back_y_last[dz].wait_recv()
        total = added(partial[dz, :, FIRST:], from_y_last[dz])
        if dz == 2:
            back_z_last[3].wait_recv()
            total = added(total, from_z_last[2])
        partial[dz, :, FIRST:] = total
        back_z_last[dz] = send(
            partial.at[dz, :, last], from_z_last.at[dz - 1], by_z[2 if dz == 2 else 1]
        )
        back_x[dz].wait_recv()
        back_y[dz].wait_recv()
        total = (
            partial[dz, here, :FIRST].astype(jnp.float32)
            + from_x[dz].astype(jnp.float32)
            + from_y[dz].astype(jnp.float32)
        )
        if dz == 2:
            back_z[3].wait_recv()
            total = total + from_z[2].astype(jnp.float32)
        partial[dz, here, :FIRST] = total.astype(jnp.bfloat16)
        back_z[dz] = send(
            partial.at[dz, here, first], from_z.at[dz - 1], by_z[2 if dz == 2 else 1]
        )

    arrive_y(0)
    arrive_z(1)
    pass_tables()
    arrive_x(0)
    arrive_y(1)
    for one in weights:
        one.wait()
    answer_rows(0)
    pass_first()
    answers_on(0)
    arrive_x(1)
    core_sum(0)
    answer_rows(1)
    pass_last()
    answers_on(1)
    arrive_y(3)
    arrive_z(2)
    x_sum(0)
    arrive_x(3)
    core_sum(1)
    arrive_y(2)
    answer_rows(3)
    answers_on(3)
    arrive_x(2)
    x_sum(1)
    answer_rows(2)
    core_sum(3)
    answers_on(2)
    core_sum(2)
    y_sum(1)
    x_sum(3)
    y_sum(3)
    x_sum(2)
    y_sum(2)
    back_y_last[0].wait_recv()
    for dz in (1, 2):
        back_z_last[dz].wait_recv()

    def last_sum(half):
        total = partial[0, half, FIRST:].astype(jnp.float32) + from_y_last[0, half].astype(
            jnp.float32
        )
        for dz in (1, 2):
            total = total + from_z_last[dz - 1, half].astype(jnp.float32)
        return total

    partial[0, there, FIRST:] = last_sum(there).astype(jnp.bfloat16)
    back_x_last = send(partial.at[0, there, last], from_x_last, by_x)
    back_x[0].wait_recv()
    back_y[0].wait_recv()
    for dz in (1, 2):
        back_z[dz].wait_recv()
    total = (
        partial[0, here, :FIRST].astype(jnp.float32)
        + from_x[0].astype(jnp.float32)
        + from_y[0].astype(jnp.float32)
    )
    for dz in (1, 2):
        total = total + from_z[dz - 1].astype(jnp.float32)
    out_ref[:FIRST] = total.astype(jnp.bfloat16)
    total = last_sum(here)
    back_x_last.wait_recv()
    out_ref[FIRST:] = (total + from_x_last[...].astype(jnp.float32)).astype(jnp.bfloat16)
    for copy in started:
        copy.wait_send()


def layer(
    lengths,
    resid,
    query,
    key_new,
    value_new,
    gain,
    slots,
    router_rows,
    cache_kv,
    w_out,
    gate_up_rows,
    w_down,
    capacity,
):
    count, width = resid.shape
    units = w_down.shape[1]
    rest = count - FIRST
    low = jnp.bfloat16
    wide = jnp.float32
    vmem = pl.BlockSpec(memory_space=pltpu.VMEM)
    hbm = pl.BlockSpec(memory_space=pl.ANY)
    block = jax.ShapeDtypeStruct((count, width), low)
    return pl.pallas_call(
        layer_kernel,
        out_shape=(block, block),
        in_specs=[pl.BlockSpec(memory_space=pltpu.SMEM)] + [vmem] * 7 + [hbm] * 4,
        out_specs=(vmem, vmem),
        scratch_shapes=[
            pltpu.VMEM(cache_kv.shape, low),
            pltpu.VMEM((2, width, width), low),
            pltpu.VMEM((count, width), low),
            pltpu.VMEM((count, width), low),
            pltpu.VMEM((count, width), low),
            pltpu.VMEM((8, count), wide),
            pltpu.VMEM((8, count), wide),
            pltpu.VMEM(slots.shape, wide),
            pltpu.VMEM(slots.shape, wide),
            pltpu.VMEM((16, 2) + slots.shape, wide),
            pltpu.VMEM((16, 2, count, width), low),
            pltpu.VMEM((16, 2, count, width), low),
            pltpu.VMEM((8, 2, count, width), low),
            pltpu.VMEM((8, FIRST, width), low),
            pltpu.VMEM((rest, width), low),
            pltpu.VMEM((4, FIRST, width), low),
            pltpu.VMEM((4, 2, rest, width), low),
            pltpu.VMEM((3, FIRST, width), low),
            pltpu.VMEM((3, 2, rest, width), low),
            pltpu.VMEM((2, units, 2 * width), low),
            pltpu.VMEM((units, 2 * width), low),
            pltpu.VMEM((BATCH * capacity, 2 * width), low),
            pltpu.VMEM((BATCH * capacity, units), low),
            pltpu.VMEM((BATCH, capacity, count), low),
            pltpu.SemaphoreType.DMA((6,)),
            pltpu.SemaphoreType.DMA((80,)),
            pltpu.SemaphoreType.DMA((80,)),
        ],
        compiler_params=pltpu.CompilerParams(
            collective_id=0, has_side_effects=True, vmem_limit_bytes=60 * 1024 * 1024
        ),
        cost_estimate=pl.CostEstimate(
            flops=12_000_000_000, bytes_accessed=18_000_000, transcendentals=2_000_000
        ),
    )(
        lengths,
        resid,
        query,
        key_new,
        value_new,
        gain,
        slots,
        router_rows,
        cache_kv,
        w_out,
        gate_up_rows,
        w_down,
    )


def slot_table(routes, experts_all):
    tokens_here = routes.shape[0]
    hits = jnp.any(
        routes.T[None, :, :] == jnp.arange(experts_all, dtype=jnp.int32)[:, None, None], axis=1
    )
    position = jnp.arange(tokens_here, dtype=jnp.int32)
    earlier = (position[:, None] < position[None, :]).astype(jnp.bfloat16)
    slots = jnp.dot(hits.astype(jnp.bfloat16), earlier, preferred_element_type=jnp.float32)
    return jnp.where(hits, slots, -1.0)


def routed_body(
    resid,
    query,
    key_new,
    value_new,
    cache_kv,
    cache_len,
    w_out,
    norm_gain,
    w_router,
    routes,
    w_gate_up,
    w_down,
):
    experts_all = w_router.shape[1]
    width = resid.shape[1]
    capacity = max(2, 8 * resid.shape[0] // lax.axis_size("ep"))
    return layer(
        cache_len,
        resid,
        query,
        key_new,
        value_new,
        norm_gain.astype(jnp.float32).reshape(1, 2 * width),
        slot_table(routes, experts_all),
        w_router.T,
        cache_kv,
        w_out,
        jnp.swapaxes(w_gate_up, 2, 3),
        w_down,
        capacity,
    )


def solution(mesh):
    fits = mesh.shape["ep"] == 16 and mesh.shape["grp"] == 2
    return jax.shard_map(
        routed_body if fits else wide_body,
        mesh=mesh,
        in_specs=(
            P("ep", "grp"),
            P("ep", "grp"),
            P("ep", "grp"),
            P("ep", "grp"),
            P(None, "ep", "grp"),
            P(),
            P("grp", None),
            P(),
            P(),
            P("ep", None),
            P("ep", None, None, "grp"),
            P("ep", "grp", None),
        ),
        out_specs=(P("ep", "grp"), P("ep", "grp")),
        check_vma=False,
    )
```
